256 devices in a mesh: ctx: 32 (over x, z), exp: 8 (over y, core).
Axes of the slice: x: 4, y: 4, z: 8, core: 2. Of those that a mesh axis runs over, the one named last changes fastest.
Arguments:
- query_in: bfloat16 [6144, 2048], P('ctx', 'exp'), may hold values from -6 to 6
- key_in: bfloat16 [6144, 2048], P('ctx', 'exp'), may hold values from -6.5 to 6.5
- value_in: bfloat16 [6144, 4096], P('ctx', 'exp'), may hold values from -6 to 6
- gate_in: bfloat16 [6144, 4096], P('ctx', 'exp'), may hold values from -6 to 6
- decay_rate: float32 [32, 6144], P('exp', 'ctx'), may hold values from 0 to 1
- beta_logit: float32 [32, 6144], P('exp', 'ctx'), may hold values from -5 to 5
- head_gain: float32 [128], replicated, may hold values from 0.5 to 1.5
- out_proj: bfloat16 [4096, 2048], P('exp'), may hold values from -0.09375 to 0.09375
- residual_in: bfloat16 [6144, 2048], P('ctx'), may hold values from -6 to 6
- post_gain: float32 [2048], replicated, may hold values from 0.5 to 1.5
- expert_ids: int32 [6144, 10], P('ctx'), may hold values from 0 to 255, all different within a row; in each aligned block of 192 rows (0 to 191, 192 to 383, ...) at most 16 rows name the same one
- route_weight: float32 [6144, 10], P('ctx'), may hold values from 0.1 to 1
- w_gate: bfloat16 [256, 2048, 512], P(('ctx', 'exp')), may hold values from -0.125 to 0.125
- w_up: bfloat16 [256, 2048, 512], P(('ctx', 'exp')), may hold values from -0.125 to 0.125
- w_down: bfloat16 [256, 512, 2048], P(('ctx', 'exp')), may hold values from -0.25 to 0.25
Outputs:
- middle: bfloat16 [6144, 2048], P('ctx', 'exp')
- layer_out: bfloat16 [6144, 2048], P('ctx', 'exp')
The draws below stay inside these ranges and needn't reach their ends.
Inputs may be any that keep to these rules, and one draw needn't show every extreme that they name: `expert_ids`: each token names 10 different experts; among the 192 rows of one device no expert is named more than 16 times.
All inputs are finite; a program needn't handle non-finite values.
Results may differ from the reference program's by a relative error of at most 0.017.
Values may be sent and summed in bfloat16 or wider, within the bound.
No kernel may reach another device: no remote copies, remote signals or barrier semaphores. Data moves between devices by JAX's collectives and lax.ppermute only.
A program may use at most 128 MiB of HBM per device.

```python
import math
import jax
import jax.numpy as jnp
import numpy as np
from jax import lax

D = 2048
VALUE_HEADS = 32
HK = 16
DK = 128
DV = 128
FFE = 512
TOP = 10
TOK_DEV = 192
WINDOW_TOKENS = 6144
EXPERTS = 256
MOST = 16


def draw_decay_rate(key, part):
    key = jax.random.fold_in(key, 11)
    token_flows = jax.random.split(key, 9)
    fast_share = 0.5
    switch_share = 0.25
    fast_heads = jax.random.uniform(token_flows[0], (VALUE_HEADS, 1)) < fast_share
    fast_rate = jnp.exp(jax.random.uniform(token_flows[1], (VALUE_HEADS, 1), minval=math.log(1.0 / 50.0), maxval=math.log(1.0 / 30.0)))
    slow_rate = jnp.exp(jax.random.uniform(token_flows[2], (VALUE_HEADS, 1), minval=math.log(0.05), maxval=math.log(0.3))) / WINDOW_TOKENS
    block_total = WINDOW_TOKENS // TOK_DEV
    switch_heads = jax.random.uniform(token_flows[7], (VALUE_HEADS, 1)) < switch_share
    switch_block = jax.random.randint(token_flows[8], (VALUE_HEADS, 1), block_total // 4, 3 * block_total // 4 + 1)
    token_block = (jnp.arange(WINDOW_TOKENS, dtype=jnp.int32) // TOK_DEV)[None, :]
    switched = jnp.logical_and(switch_heads, token_block >= switch_block)
    base_level = jnp.where(jnp.logical_or(fast_heads, switched), fast_rate, slow_rate)
    dispersion = jnp.exp(jax.random.uniform(token_flows[3], (VALUE_HEADS, block_total, 1), minval=math.log(0.5), maxval=math.log(2.0)))
    dispersion = jnp.broadcast_to(dispersion, (VALUE_HEADS, block_total, TOK_DEV)).reshape(VALUE_HEADS, WINDOW_TOKENS)
    jagged_noise = jax.random.uniform(token_flows[4], (VALUE_HEADS, WINDOW_TOKENS), minval=0.5, maxval=1.5)
    surge_position = jax.random.uniform(token_flows[5], (1, WINDOW_TOKENS)) < 4.0 / WINDOW_TOKENS
    surge_length = jax.random.uniform(token_flows[6], (VALUE_HEADS, WINDOW_TOKENS), minval=0.22, maxval=0.69)
    return (base_level * dispersion * jagged_noise + jnp.where(surge_position, surge_length, 0.0)).astype(jnp.float32)


def draw_key_in(key, part):
    key = jax.random.fold_in(key, 23)
    key_flows = jax.random.split(key, 4)
    group_width = DK // 16
    coordinate_order = jax.random.permutation(key_flows[0], DK).astype(jnp.int32)
    head_offset = jax.random.randint(key_flows[1], (HK,), 0, 16)
    token_block = jnp.arange(WINDOW_TOKENS, dtype=jnp.int32) // TOK_DEV
    group_now = (token_block[:, None] + head_offset[None, :]) % 16
    active = (coordinate_order // group_width)[None, None, :] == group_now[:, :, None]
    main_part = jnp.clip(jax.random.normal(key_flows[2], (WINDOW_TOKENS, HK, DK)), -6.0, 6.0)
    background = 0.05 * jnp.clip(jax.random.normal(key_flows[3], (WINDOW_TOKENS, HK, DK)), -6.0, 6.0)
    return (jnp.where(active, main_part, 0.0) + background).reshape(WINDOW_TOKENS, HK * DK).astype(jnp.bfloat16)


def level_of(stream_key, dims, shards, least, top_value):
    def one(position, shards_of):
        steps = jax.random.uniform(jax.random.fold_in(jax.random.fold_in(stream_key, 6), position), (shards_of,), jnp.float32, least / len(shards), top_value / len(shards))
        return jnp.repeat(jnp.exp(steps), dims[position] // shards_of).reshape((-1,) + (1,) * (len(dims) - position - 1))

    loudness = one(*shards[0])
    for cut in shards[1:]:
        loudness = loudness * one(*cut)
    return loudness


def routed_block(stream_key, own, number, rows, number_of, top, bound, skew):
    sequence = jax.random.permutation(stream_key, number_of)
    packed, usual = portions_of(number_of, rows * top, bound, skew, True), portions_of(number_of, rows * top, bound, skew, False)
    places = jnp.arange(number_of)

    def named(lengths, offset_by):
        used = int((lengths > 0).sum())
        fixed = max(1, used // 4)
        moved = fixed + (places - fixed + offset_by * (used - fixed)) % max(1, number_of - fixed)
        return jnp.zeros((number_of,), jnp.int32).at[sequence[jnp.where(places < fixed, places, moved)]].set(jnp.asarray(lengths, jnp.int32))

    lengths = jnp.where(number % 4 == 0, named(packed, number // 4), named(usual, number - number // 4 - 1))
    mixed = jax.random.permutation(jax.random.fold_in(own, 3), number_of)
    giver, sink = mixed[0:number_of // 2 * 2:2], mixed[1:number_of // 2 * 2:2]
    margin = jnp.minimum(lengths[giver] - 1, bound - lengths[sink]) // 2
    margin = jnp.where((giver == sequence[0]) | (sink == sequence[0]) | (lengths[sink] == 0), 0, jnp.maximum(margin, 0))
    moved = jax.random.randint(jax.random.fold_in(own, 4), (number_of // 2,), 0, 1 << 20) % (margin + 1)
    lengths = lengths.at[giver].add(-moved).at[sink].add(moved)
    labels = jnp.searchsorted(jnp.cumsum(lengths), jnp.arange(rows * top), side="right").astype(jnp.int32)
    listing = labels.reshape(top, rows).T
    listing = listing[jax.random.permutation(jax.random.fold_in(own, 1), rows)]
    offset_by = jax.random.randint(jax.random.fold_in(own, 2), (rows, 1), 0, top)
    return jnp.take_along_axis(listing, (jnp.arange(top)[None, :] + offset_by) % top, axis=1)


def portions_of(amount, total, limit, skew, full):
    loads = [(1 << 20) // math.isqrt(standing ** skew) + 1 for standing in range(1, amount + 1)]
    largest = limit if full else min(limit, max(-(-total // amount), total * loads[0] // sum(loads)))
    least = 1 if total - largest >= amount - 1 else 0
    counts, spare = [largest] + [least] * (amount - 1), total - largest - least * (amount - 1)
    while spare > 0:
        free = [i for i in range(1, amount) if counts[i] < largest] or [i for i in range(1, amount) if counts[i] < limit]
        pool, budget = sum([loads[i] for i in free]), spare
        for i in free:
            extra = min(limit - counts[i], max(1, budget * loads[i] // pool), spare)
            counts[i] = counts[i] + extra
            spare = spare - extra
    return np.array(counts)


def noise(own_key, extent, spread, bound, cuts=(), kind=jnp.bfloat16):
    result = spread * jax.random.normal(own_key, extent, jnp.float32)
    if cuts:
        result = result * level_of(own_key, extent, cuts, -0.22, 0.18)
    return jnp.clip(result, -bound, bound).astype(kind)


def setup_inputs(seed: int = 0) -> dict:
    splits = jax.random.split(jax.random.key(seed), 16)
    query_in = noise(splits[0], (WINDOW_TOKENS, HK * DK), 1.0, 6.0, ((0, 32), (1, 8)))
    key_in = draw_key_in(jax.random.fold_in(splits[15], 71), 0)
    value_in = noise(splits[2], (WINDOW_TOKENS, VALUE_HEADS * DV), 1.0, 6.0, ((0, 32), (1, 8)))
    gate_in = noise(splits[3], (WINDOW_TOKENS, VALUE_HEADS * DV), 1.0, 6.0, ((0, 32), (1, 8)))
    decay_rate = draw_decay_rate(jax.random.fold_in(splits[15], 71), 0)
    beta_logit = noise(splits[5], (VALUE_HEADS, WINDOW_TOKENS), 1.0, 5.0, ((0, 8), (1, 32)), jnp.float32)
    head_gain = jnp.clip(1.0 + 0.1 * jax.random.normal(splits[6], (DV,), jnp.float32), 0.5, 1.5)
    out_proj = noise(splits[7], (VALUE_HEADS * DV, D), (VALUE_HEADS * DV) ** -0.5, 0.09375, ((0, 8),))
    residual_in = noise(splits[8], (WINDOW_TOKENS, D), 1.0, 6.0, ((0, 32),))
    post_gain = jnp.clip(1.0 + 0.1 * jax.random.normal(splits[9], (D,), jnp.float32), 0.5, 1.5)
    expert_ids_keys = jax.random.split(jax.random.fold_in(splits[10], 1), WINDOW_TOKENS // TOK_DEV)
    expert_ids_turns = jax.random.permutation(jax.random.fold_in(splits[10], 3), WINDOW_TOKENS // TOK_DEV)
    expert_ids = jax.vmap(lambda own, number: routed_block(jax.random.fold_in(splits[10], 2), own, number, TOK_DEV, EXPERTS, TOP, MOST, 2))(expert_ids_keys, expert_ids_turns).reshape((WINDOW_TOKENS, TOP))
    route_weight = jnp.clip(0.1 + 0.9 * jax.random.uniform(splits[11], (WINDOW_TOKENS, TOP), jnp.float32) ** level_of(splits[11], (WINDOW_TOKENS, TOP), ((0, 32),), -0.2, 0.2), 0.1, 1.0)
    w_gate = noise(splits[12], (EXPERTS, D, FFE), D ** -0.5, 0.125, ((0, 256),))
    w_up = noise(splits[13], (EXPERTS, D, FFE), D ** -0.5, 0.125, ((0, 256),))
    w_down = noise(splits[14], (EXPERTS, FFE, D), FFE ** -0.5, 0.25, ((0, 256),))
    return {"query_in": query_in, "key_in": key_in, "value_in": value_in, "gate_in": gate_in, "decay_rate": decay_rate, "beta_logit": beta_logit, "head_gain": head_gain, "out_proj": out_proj, "residual_in": residual_in, "post_gain": post_gain, "expert_ids": expert_ids, "route_weight": route_weight, "w_gate": w_gate, "w_up": w_up, "w_down": w_down}


highest = lax.Precision.HIGHEST
eps_small = 1e-06

def unit_rows(field):
    return field * lax.rsqrt(lax.optimization_barrier(jnp.sum(field * field, axis=-1, keepdims=True)) + eps_small)

def delta_rule(queries, keys_all, values, decays, update_rate):

    def advance(carried_state, inputs_t):
        query_t, key_t, value_t, decay_t, rate_t = inputs_t
        decayed = carried_state * jnp.exp(-decay_t)[:, None, None]
        predicted = jnp.einsum('hvk,hk->hv', decayed, key_t, precision=highest)
        written = rate_t[:, None] * (value_t - predicted)
        carried_state = decayed + jnp.einsum('hv,hk->hvk', written, key_t, precision=highest)
        return (carried_state, jnp.einsum('hvk,hk->hv', carried_state, query_t, precision=highest))
    initial = jnp.zeros((VALUE_HEADS, DV, DK), jnp.float32)
    _, outputs = lax.scan(advance, initial, (queries, keys_all, values, decays, update_rate))
    return outputs

def moe_sum(normed, expert_ids, route_weight, w_gate, w_up, w_down):
    token_total, top_count = expert_ids.shape
    flat_ids = expert_ids.reshape(-1)
    pair_order = jnp.argsort(flat_ids, stable=True).astype(jnp.int32)
    ranked = flat_ids[pair_order]
    numbers = jnp.arange(EXPERTS, dtype=jnp.int32)
    starts = jnp.searchsorted(ranked, numbers, side='left').astype(jnp.int32)
    finish = jnp.searchsorted(ranked, numbers, side='right').astype(jnp.int32)
    flat_weight = route_weight.reshape(-1)
    block_len = 64

    def per_expert(expert, accumulated):
        first_slot = starts[expert]
        last_slot = finish[expert]

        def per_block(block_index, inner):
            slot_index = first_slot + block_index * block_len + jnp.arange(block_len, dtype=jnp.int32)
            usable = slot_index < last_slot
            pair_index = pair_order[jnp.minimum(slot_index, token_total * top_count - 1)]
            token_index = (pair_index // top_count).astype(jnp.int32)
            row_block = normed[token_index]
            gate_act = jnp.dot(row_block, w_gate[expert], preferred_element_type=jnp.float32)
            up_act = jnp.dot(row_block, w_up[expert], preferred_element_type=jnp.float32)
            hidden = (jax.nn.silu(gate_act) * up_act).astype(jnp.bfloat16)
            produced = jnp.dot(hidden, w_down[expert], preferred_element_type=jnp.float32).astype(jnp.bfloat16)
            produced = lax.optimization_barrier(produced).astype(jnp.float32)
            weighting = jnp.where(usable, flat_weight[pair_index], 0.0)
            return inner.at[token_index].add(produced * weighting[:, None])
        blocks_needed = (last_slot - first_slot + block_len - 1) // block_len
        return lax.fori_loop(0, blocks_needed, per_block, accumulated)
    return lax.fori_loop(0, EXPERTS, per_expert, jnp.zeros((token_total, D), jnp.float32))

def reference(query_in, key_in, value_in, gate_in, decay_rate, beta_logit, head_gain, out_proj, residual_in, post_gain, expert_ids, route_weight, w_gate, w_up, w_down):
    group_ratio = VALUE_HEADS // HK
    queries = unit_rows(query_in.astype(jnp.float32).reshape(WINDOW_TOKENS, HK, DK)) * DK ** (-0.5)
    keys_all = unit_rows(key_in.astype(jnp.float32).reshape(WINDOW_TOKENS, HK, DK))
    queries = jnp.repeat(queries, group_ratio, axis=1)
    keys_all = jnp.repeat(keys_all, group_ratio, axis=1)
    values = value_in.astype(jnp.float32).reshape(WINDOW_TOKENS, VALUE_HEADS, DV)
    update_rate = jax.nn.sigmoid(beta_logit).T
    outputs = delta_rule(queries, keys_all, values, decay_rate.T, update_rate)
    scaling = lax.rsqrt(lax.optimization_barrier(jnp.mean(outputs * outputs, axis=-1, keepdims=True)) + eps_small)
    gate_act = jax.nn.silu(gate_in.astype(jnp.float32).reshape(WINDOW_TOKENS, VALUE_HEADS, DV))
    gated = (outputs * scaling * head_gain * gate_act).astype(jnp.bfloat16).reshape(WINDOW_TOKENS, VALUE_HEADS * DV)
    mixed = jnp.dot(gated, out_proj, preferred_element_type=jnp.float32)
    middle = (residual_in.astype(jnp.float32) + mixed).astype(jnp.bfloat16)
    held_rows = lax.optimization_barrier(middle).astype(jnp.float32)
    normed = (held_rows * lax.rsqrt(lax.optimization_barrier(jnp.mean(held_rows * held_rows, axis=-1, keepdims=True)) + eps_small) * post_gain).astype(jnp.bfloat16)
    expert_mix = moe_sum(normed, expert_ids, route_weight, w_gate, w_up, w_down)
    return (middle, (held_rows + expert_mix).astype(jnp.bfloat16))
```

```python
import functools

import jax
import jax.numpy as jnp
from jax import lax
from jax.experimental import pallas as pl
from jax.experimental.pallas import tpu as pltpu
from jax.sharding import Mesh, PartitionSpec as P

DK = 128
DV = 128
SLOTS = 16
EPS = 1e-06
BF = jnp.bfloat16
F32 = jnp.float32
NN = ((1,), (0,))
NT = ((1,), (1,))
TN = ((0,), (0,))
VMEM_BYTES = 50 * 1024 * 1024


def mm(left, right, dims=NN):
    return lax.dot_general(
        left.astype(BF), right.astype(BF), (dims, ((), ())), preferred_element_type=F32
    )


def exact(left, right, dims=NN):
    return lax.dot_general(
        left, right, (dims, ((), ())), precision=lax.Precision.HIGHEST, preferred_element_type=F32
    )


def halves(value):
    high = value.astype(BF)
    return high, (value - high.astype(F32)).astype(BF)


def mm3(left, right, dims=NN):
    left_high, left_low = halves(left)
    right_high, right_low = halves(right)
    return (
        mm(left_high, right_high, dims)
        + mm(left_high, right_low, dims)
        + mm(left_low, right_high, dims)
    )


def silu(value):
    return value / (1.0 + jnp.exp(-value))


def call(kernel, out_shape, *operands, flops=0, moved=0, **more):
    return pl.pallas_call(
        kernel,
        out_shape=out_shape,
        compiler_params=pltpu.CompilerParams(vmem_limit_bytes=VMEM_BYTES),
        cost_estimate=pl.CostEstimate(flops=flops, bytes_accessed=moved, transcendentals=0),
        **more,
    )(*operands)


def mixer_kernel(q_ref, k_ref, v_ref, decay_ref, logit_ref, c_ref, b_ref, inside_ref, reach_ref):
    length = q_ref.shape[0]
    heads = decay_ref.shape[0]
    ratio = heads // (q_ref.shape[1] // DK)
    row = lax.broadcasted_iota(jnp.int32, (length, length), 0)
    col = lax.broadcasted_iota(jnp.int32, (length, length), 1)
    on = row >= col
    below = row > col
    eye = jnp.where(row == col, 1.0, 0.0)
    tri = jnp.where(on, 1.0, 0.0)
    rate_row = 1.0 / (1.0 + jnp.exp(-logit_ref[...]))
    log_row = -exact(decay_ref[...], tri, NT)
    log_col = -exact(tri, decay_ref[...], NT)
    rate_col = exact(eye, rate_row, NT)
    ones = jnp.ones((8, DK), F32)
    systems, weights, scales = [], [], []
    for group in range(heads // ratio):
        part = slice(group * DK, (group + 1) * DK)
        query = q_ref[:, part]
        key = k_ref[:, part]
        query_f = query.astype(F32)
        key_f = key.astype(F32)
        query_scale = lax.rsqrt(jnp.sum(query_f * query_f, axis=1, keepdims=True) + EPS) * DK**-0.5
        key_scale = lax.rsqrt(jnp.sum(key_f * key_f, axis=1, keepdims=True) + EPS)
        key_scale_row = lax.rsqrt(exact(ones, key_f * key_f, NT)[:1] + EPS)
        key_key = mm(key, key, NT) * (key_scale * key_scale_row)
        query_key = mm(query, key, NT) * (query_scale * key_scale_row)
        for head in range(group * ratio, (group + 1) * ratio):
            apart = jnp.where(on, log_col[:, head : head + 1] - log_row[head : head + 1, :], 0.0)
            fading = jnp.where(on, jnp.exp(apart), 0.0) * rate_row[head : head + 1, :]
            systems.append(jnp.where(below, key_key * fading, 0.0))
            weights.append(query_key * fading)
            scales.append((query_f * query_scale, key_f * key_scale, key_scale, key))
    inverses = [eye - jnp.where(row // 2 == col // 2, system, 0.0) for system in systems]
    size = 2
    while size < length:
        lower = (row // (2 * size) == col // (2 * size)) & (row // size > col // size)
        crossing = [
            mm(jnp.where(lower, system, 0.0), inverse)
            for system, inverse in zip(systems, inverses)
        ]
        inverses = [
            inverse - mm(inverse, cross) for inverse, cross in zip(inverses, crossing)
        ]
        size *= 2
    for head in range(heads):
        query_n, key_n, key_scale, key = scales[head]
        lead = jnp.exp(log_col[:, head : head + 1])
        value = v_ref[:, head * DV : (head + 1) * DV].astype(F32)
        target = jnp.concatenate([value, lead * key_n], axis=1)
        solved = mm(inverses[head], target)
        missing = target - solved - mm3(systems[head], solved)
        solved = solved + mm(inverses[head], missing)
        both = mm3(weights[head], solved)
        inside_ref[head] = both[:, :DV]
        reach_ref[head] = (lead * query_n - both[:, DV:]).astype(reach_ref.dtype)
        last = log_col[length - 1 : length, head : head + 1]
        tail = jnp.exp(last - log_col[:, head : head + 1]) * rate_col[:, head : head + 1] * key_scale
        high, low = halves(solved * tail)
        written = mm(high, key, TN) + mm(low, key, TN)
        c_ref[head] = written[DV:].astype(c_ref.dtype)
        b_ref[head] = written[:DV].astype(b_ref.dtype)


def scan_kernel(got_ref, enter_ref):
    blocks = got_ref.shape[0]
    rows = enter_ref.shape[1]
    state = jnp.zeros((rows, DK), F32)
    for block in range(blocks):
        enter_ref[block] = state.astype(BF)
        if block == blocks - 1:
            break
        removed = got_ref[block, :DK, :]
        added = got_ref[block, DK : DK + rows, :].astype(F32)
        marks = got_ref[block, DK + rows : DK + 2 * rows, :].astype(F32)
        fade = marks[0:1, :] + marks[1:2, :] + marks[2:3, :]
        high, low = halves(state)
        state = fade * state - (mm(high, removed) + mm(low, removed)) + added


def output_kernel(inside_ref, reach_ref, state_ref, gate_ref, gain_ref, proj_ref, out_ref):
    heads = inside_ref.shape[0]
    gated = []
    for head in range(heads):
        part = slice(head * DV, (head + 1) * DV)
        output = inside_ref[head] + mm(reach_ref[head], state_ref[head], NT)
        scaling = lax.rsqrt(jnp.mean(output * output, axis=1, keepdims=True) + EPS)
        opened = silu(gate_ref[:, part].astype(F32))
        gated.append((output * scaling * gain_ref[...] * opened).astype(BF))
    mixed = mm(jnp.concatenate(gated, axis=1), proj_ref[...])
    width = out_ref.shape[2]
    for share in range(out_ref.shape[0]):
        out_ref[share] = mixed[:, share * width : (share + 1) * width].astype(out_ref.dtype)


def route_kernel(ids_ref, ids_t_ref, weight_ref, pick_ref, mix_ref):
    blocks, length, top = ids_ref.shape
    slots = pick_ref.shape[1]
    targets = slots // SLOTS
    iota = lambda shape, dim: lax.broadcasted_iota(jnp.int32, shape, dim)
    earlier = (iota((length, length), 0) > iota((length, length), 1)).astype(BF)
    earlier_t = (iota((length, length), 0) < iota((length, length), 1)).astype(BF)
    spread = (iota((targets, slots), 1) // SLOTS == iota((targets, slots), 0)).astype(BF)
    spread_t = (iota((slots, targets), 0) // SLOTS == iota((slots, targets), 1)).astype(BF)
    number = iota((length, targets), 1)
    number_t = iota((targets, length), 0)
    slot = (iota((length, slots), 1) % SLOTS).astype(F32)
    slot_t = (iota((slots, length), 0) % SLOTS).astype(F32)

    def one(block, _):
        ids = ids_ref[block]
        ids_t = ids_t_ref[block]
        weight = weight_ref[block]
        named = jnp.zeros((length, targets), F32)
        wide = jnp.zeros((length, targets), F32)
        named_t = jnp.zeros((targets, length), F32)
        for choice in range(top):
            hit = ids[:, choice : choice + 1] == number
            named = named + jnp.where(hit, 1.0, 0.0)
            wide = wide + jnp.where(hit, weight[:, choice : choice + 1], 0.0)
            named_t = named_t + jnp.where(ids_t[choice : choice + 1, :] == number_t, 1.0, 0.0)
        place = jnp.where(named > 0.0, mm(earlier, named), -1.0)
        place_t = jnp.where(named_t > 0.0, mm(named_t, earlier_t), -1.0)
        mix_ref[block] = jnp.where(mm(place, spread) == slot, mm(wide, spread), 0.0).astype(BF)
        pick_ref[block] = jnp.where(mm(spread_t, place_t) == slot_t, 1.0, 0.0).astype(BF)
        return 0

    lax.fori_loop(0, blocks, one, 0)


def pick_kernel(pick_ref, token_ref, send_ref):
    targets = send_ref.shape[0]
    width = send_ref.shape[2]
    for block in range(pick_ref.shape[0]):
        rows = mm(pick_ref[block], token_ref[block]).astype(BF)
        send_ref[:, block * SLOTS : (block + 1) * SLOTS, :] = rows.reshape(targets, SLOTS, width)


def expert_kernel(rows_ref, gain_ref, gate_ref, up_ref, down_ref, out_ref, normed_ref):
    groups, shares, count, width = rows_ref.shape
    for group in range(groups):
        place = slice(group * count, (group + 1) * count)
        total = jnp.zeros((count, 1), F32)
        for share in range(shares):
            piece = rows_ref[group, share].astype(F32)
            total = total + jnp.sum(piece * piece, axis=1, keepdims=True)
        scaling = lax.rsqrt(total / (shares * width) + EPS)
        for share in range(shares):
            part = slice(share * width, (share + 1) * width)
            piece = rows_ref[group, share].astype(F32)
            normed_ref[place, part] = (piece * scaling * gain_ref[:, part]).astype(BF)
    normed = normed_ref[...]
    hidden = (silu(mm(normed, gate_ref[...])) * mm(normed, up_ref[...])).astype(BF)
    for share in range(shares):
        part = slice(share * width, (share + 1) * width)
        produced = mm(hidden, down_ref[:, part]).astype(BF)
        for group in range(groups):
            out_ref[group, share] = produced[group * count : (group + 1) * count]


def combine_kernel(mix_ref, rows_ref, out_ref):
    targets, _, width = rows_ref.shape
    for block in range(mix_ref.shape[0]):
        rows = rows_ref[:, block * SLOTS : (block + 1) * SLOTS, :].reshape(targets * SLOTS, width)
        out_ref[block] = mm(mix_ref[block], rows).astype(out_ref.dtype)


def swap(value, axes):
    return lax.all_to_all(value, axes, 0, 0, tiled=True)


def on_device(
    query_in,
    key_in,
    value_in,
    gate_in,
    decay_rate,
    beta_logit,
    head_gain,
    out_proj,
    residual_in,
    post_gain,
    expert_ids,
    route_weight,
    w_gate,
    w_up,
    w_down,
):
    length = query_in.shape[0]
    heads = decay_rate.shape[0]
    blocks = lax.axis_size("z")
    groups = lax.axis_size("x")
    shares = lax.axis_size("y") * lax.axis_size("c")
    share = lax.axis_index(("y", "c"))
    width = residual_in.shape[1] // shares
    count = blocks * SLOTS
    targets = groups * shares
    shape = jax.ShapeDtypeStruct

    all_ids = lax.all_gather(expert_ids, "z")
    all_weight = lax.all_gather(route_weight, "z")
    own = (all_ids // shares) % blocks == lax.axis_index("z")
    local_ids = jnp.where(own, (all_ids // (blocks * shares)) * shares + all_ids % shares, -1)
    pick, mix = call(
        route_kernel,
        (
            shape((blocks, targets * SLOTS, length), BF),
            shape((blocks, length, targets * SLOTS), BF),
        ),
        local_ids,
        jnp.swapaxes(local_ids, 1, 2),
        all_weight,
    )

    removed, added, inside, reach = call(
        mixer_kernel,
        (
            shape((heads, DK, DK), BF),
            shape((heads, DV, DK), BF),
            shape((heads, length, DV), F32),
            shape((heads, length, DK), BF),
        ),
        query_in,
        key_in,
        value_in,
        decay_rate,
        beta_logit,
    )
    ctx = groups * blocks
    cuts = ctx // heads
    rows = DV // cuts
    fade = jnp.exp(-jnp.sum(decay_rate, axis=1))
    first, second = halves(fade)
    third = (fade - first.astype(F32) - second.astype(F32)).astype(BF)
    marks = jnp.stack([first, second, third] + [jnp.zeros_like(first)] * (rows - 3), axis=1)
    marks = jnp.broadcast_to(marks[:, None, :, None], (heads, cuts, rows, DK))
    send = jnp.concatenate(
        [
            jnp.broadcast_to(removed[:, None], (heads, cuts, DK, DK)),
            added.reshape(heads, cuts, rows, DK),
            marks,
        ],
        axis=2,
    ).reshape(ctx, DK + 2 * rows, DK)
    got = swap(send, ("x", "z"))
    enter = call(scan_kernel, shape((ctx, rows, DK), BF), got)
    state = swap(enter, ("x", "z")).reshape(heads, DV, DK)

    partial = call(
        output_kernel,
        shape((shares, length, width), BF),
        inside,
        reach,
        state,
        gate_in,
        head_gain.reshape(1, DV),
        out_proj,
    )
    mixed = jnp.sum(swap(partial, ("y", "c")).astype(F32), axis=0)
    residual = lax.dynamic_slice_in_dim(residual_in, share * width, width, 1)
    middle = (residual.astype(F32) + mixed).astype(BF)

    tokens = lax.all_gather(middle, "z")
    send = call(pick_kernel, shape((targets, count, width), BF), pick, tokens)
    arrived = swap(send, ("x", "y", "c")).reshape(groups, shares, count, width)
    produced = call(
        expert_kernel,
        shape((groups, shares, count, width), BF),
        arrived,
        post_gain.reshape(1, -1),
        w_gate[0],
        w_up[0],
        w_down[0],
        scratch_shapes=[pltpu.VMEM((groups * count, shares * width), BF)],
    )
    returned = swap(produced.reshape(targets, count, width), ("x", "y", "c"))
    mixes = call(combine_kernel, shape((blocks, length, width), BF), mix, returned)
    expert_mix = jnp.sum(swap(mixes, "z").astype(F32), axis=0)
    layer_out = (middle.astype(F32) + expert_mix).astype(BF)
    return (middle, layer_out)


def solution(mesh):
    ctx, exp = mesh.devices.shape
    split = Mesh(mesh.devices.reshape(4, ctx // 4, exp // 2, 2), ("x", "z", "y", "c"))
    row, col = ("x", "z"), ("y", "c")
    in_specs = (
        P(row, col),
        P(row, col),
        P(row, col),
        P(row, col),
        P(col, row),
        P(col, row),
        P(),
        P(col, None),
        P(row, None),
        P(),
        P(row, None),
        P(row, None),
        P(row + col, None, None),
        P(row + col, None, None),
        P(row + col, None, None),
    )
    out_specs = (P(row, col), P(row, col))
    return jax.shard_map(
        on_device, mesh=split, in_specs=in_specs, out_specs=out_specs, check_vma=False
    )
```

```python
import functools

import jax
import jax.numpy as jnp
from jax import lax
from jax.experimental import pallas as pl
from jax.experimental.pallas import tpu as pltpu
from jax.sharding import Mesh, PartitionSpec as P

DK = 128
DV = 128
SLOTS = 16
MARKS = 16
TARGETS = 32
SHARES = 8
EPS = 1e-06
BF = jnp.bfloat16
F32 = jnp.float32
NN = ((1,), (0,))
NT = ((1,), (1,))
TN = ((0,), (0,))
VMEM_BYTES = 50 * 1024 * 1024


def mm(left, right, dims=NN):
    return lax.dot_general(
        left.astype(BF), right.astype(BF), (dims, ((), ())), preferred_element_type=F32
    )


def exact(left, right, dims=NN):
    return lax.dot_general(
        left, right, (dims, ((), ())), precision=lax.Precision.HIGHEST, preferred_element_type=F32
    )


def halves(value):
    high = value.astype(BF)
    return high, (value - high.astype(F32)).astype(BF)


def mm3(left, right, dims=NN):
    left_high, left_low = halves(left)
    right_high, right_low = halves(right)
    return (
        mm(left_high, right_high, dims)
        + mm(left_high, right_low, dims)
        + mm(left_low, right_high, dims)
    )


def pieces(value):
    first, second = halves(value)
    third = (value - first.astype(F32) - second.astype(F32)).astype(BF)
    row = lax.broadcasted_iota(jnp.int32, value.shape, 0)
    return jnp.where(row == 0, first, jnp.where(row == 1, second, third))


def joined(marks):
    marks = marks.astype(F32)
    return marks[0:1] + marks[1:2] + marks[2:3]


def unpack(got, rows):
    fade = joined(got[DK + rows : DK + rows + MARKS, :])
    return got[:DK, :], got[DK : DK + rows, :].astype(F32), fade


def advance(state, removed, fade):
    high, low = halves(state)
    return fade * state - (mm(high, removed) + mm(low, removed))


def silu(value):
    return value / (1.0 + jnp.exp(-value))


def call(kernel, out_shape, *operands, flops=0, moved=0, **more):
    return pl.pallas_call(
        kernel,
        out_shape=out_shape,
        compiler_params=pltpu.CompilerParams(vmem_limit_bytes=VMEM_BYTES),
        cost_estimate=pl.CostEstimate(flops=flops, bytes_accessed=moved, transcendentals=0),
        **more,
    )(*operands)


def mixer_kernel(
    q_ref, k_ref, v_ref, decay_ref, logit_ref, ids_ref, weight_ref, send_ref, inside_ref, reach_ref
):
    length = q_ref.shape[0]
    heads = decay_ref.shape[0]
    ratio = heads // (q_ref.shape[1] // DK)
    places = send_ref.shape[0]
    cuts = places // heads
    rows = DV // cuts
    targets = TARGETS
    shares = SHARES
    row = lax.broadcasted_iota(jnp.int32, (length, length), 0)
    col = lax.broadcasted_iota(jnp.int32, (length, length), 1)
    on = row >= col
    below = row > col
    eye = jnp.where(row == col, 1.0, 0.0)
    tri = jnp.where(on, 1.0, 0.0)
    rate_row = 1.0 / (1.0 + jnp.exp(-logit_ref[...]))
    log_row = -exact(decay_ref[...], tri, NT)
    log_col = -exact(tri, decay_ref[...], NT)
    rate_col = exact(eye, rate_row, NT)
    ones = jnp.ones((8, DK), F32)
    systems, weights, scales = [], [], []
    for group in range(heads // ratio):
        part = slice(group * DK, (group + 1) * DK)
        query = q_ref[:, part]
        key = k_ref[:, part]
        query_f = query.astype(F32)
        key_f = key.astype(F32)
        query_scale = lax.rsqrt(jnp.sum(query_f * query_f, axis=1, keepdims=True) + EPS) * DK**-0.5
        key_scale = lax.rsqrt(jnp.sum(key_f * key_f, axis=1, keepdims=True) + EPS)
        key_scale_row = lax.rsqrt(exact(ones, key_f * key_f, NT)[:1] + EPS)
        key_key = mm(key, key, NT) * (key_scale * key_scale_row)
        query_key = mm(query, key, NT) * (query_scale * key_scale_row)
        for head in range(group * ratio, (group + 1) * ratio):
            apart = jnp.where(on, log_col[:, head : head + 1] - log_row[head : head + 1, :], 0.0)
            fading = jnp.where(on, jnp.exp(apart), 0.0) * rate_row[head : head + 1, :]
            systems.append(jnp.where(below, key_key * fading, 0.0))
            weights.append(query_key * fading)
            scales.append((query_f * query_scale, key_f * key_scale, key_scale, key))
    inverses = [eye - jnp.where(row // 2 == col // 2, system, 0.0) for system in systems]
    size = 2
    while size < length:
        lower = (row // (2 * size) == col // (2 * size)) & (row // size > col // size)
        crossing = [
            mm(jnp.where(lower, system, 0.0), inverse)
            for system, inverse in zip(systems, inverses)
        ]
        inverses = [
            inverse - mm(inverse, cross) for inverse, cross in zip(inverses, crossing)
        ]
        size *= 2
    for head in range(heads):
        query_n, key_n, key_scale, key = scales[head]
        lead = jnp.exp(log_col[:, head : head + 1])
        value = v_ref[:, head * DV : (head + 1) * DV].astype(F32)
        target = jnp.concatenate([value, lead * key_n], axis=1)
        solved = mm(inverses[head], target)
        missing = target - solved - mm3(systems[head], solved)
        solved = solved + mm(inverses[head], missing)
        both = mm3(weights[head], solved)
        inside_ref[head] = both[:, :DV]
        reach_ref[head] = (lead * query_n - both[:, DV:]).astype(reach_ref.dtype)
        last = log_col[length - 1 : length, head : head + 1]
        tail = jnp.exp(last - log_col[:, head : head + 1]) * rate_col[:, head : head + 1] * key_scale
        high, low = halves(solved * tail)
        written = mm(high, key, TN) + mm(low, key, TN)
        removed = written[DV:].astype(BF)
        added = written[:DV].astype(BF)
        fade = pieces(jnp.broadcast_to(jnp.exp(last), (MARKS, DK)))
        for cut in range(cuts):
            place = head * cuts + cut
            send_ref[place, :DK, :] = removed
            send_ref[place, DK : DK + rows, :] = added[cut * rows : (cut + 1) * rows]
            send_ref[place, DK + rows : DK + rows + MARKS, :] = fade
    base = DK + rows + MARKS
    number = lax.broadcasted_iota(jnp.int32, (targets, length), 0)
    number = (number // shares) * (places * shares) + number % shares
    for place in range(places):
        weight = jnp.zeros((targets, length), F32)
        for choice in range(ids_ref.shape[0]):
            hit = ids_ref[choice : choice + 1, :] == number + place * shares
            weight = weight + jnp.where(hit, weight_ref[choice : choice + 1, :], 0.0)
        weight = weight.astype(BF)
        send_ref[place, base : base + targets, :] = weight[:, :DK]
        send_ref[place, base + targets :, :] = jnp.concatenate(
            [weight[: targets // 2, DK:], weight[targets // 2 :, DK:]], axis=1
        )


def total_kernel(got_ref, total_ref):
    blocks = got_ref.shape[0]
    rows = total_ref.shape[0] - DK - MARKS
    row = lax.broadcasted_iota(jnp.int32, (DK, DK), 0)
    col = lax.broadcasted_iota(jnp.int32, (DK, DK), 1)
    eye = jnp.where(row == col, 1.0, 0.0)
    whole = jnp.ones((1, DK), F32)
    product = eye
    state = jnp.zeros((rows, DK), F32)
    for block in range(blocks):
        removed, added, fade = unpack(got_ref[block], rows)
        if block == 0:
            product = fade * eye - removed.astype(F32)
            state = added
        else:
            product = advance(product, removed, fade)
            state = advance(state, removed, fade) + added
        whole = whole * fade
    total_ref[:DK, :] = (whole * eye - product).astype(BF)
    total_ref[DK : DK + rows, :] = state.astype(BF)
    total_ref[DK + rows :, :] = pieces(jnp.broadcast_to(whole, (MARKS, DK)))


def state_kernel(here_ref, total_ref, got_ref, enter_ref):
    blocks, rows, _ = enter_ref.shape
    state = jnp.zeros((rows, DK), F32)
    for group in range(total_ref.shape[0] - 1):
        removed, added, fade = unpack(total_ref[group], rows)
        state = jnp.where(group < here_ref[0], advance(state, removed, fade) + added, state)
    for block in range(blocks):
        enter_ref[block] = state.astype(BF)
        if block < blocks - 1:
            removed, added, fade = unpack(got_ref[block], rows)
            state = advance(state, removed, fade) + added


def output_kernel(inside_ref, reach_ref, state_ref, gate_ref, gain_ref, proj_ref, out_ref):
    heads = inside_ref.shape[0]
    gated = []
    for head in range(heads):
        part = slice(head * DV, (head + 1) * DV)
        output = inside_ref[head] + mm(reach_ref[head], state_ref[head], NT)
        scaling = lax.rsqrt(jnp.mean(output * output, axis=1, keepdims=True) + EPS)
        opened = silu(gate_ref[:, part].astype(F32))
        gated.append((output * scaling * gain_ref[...] * opened).astype(BF))
    mixed = mm(jnp.concatenate(gated, axis=1), proj_ref[...])
    width = out_ref.shape[2]
    for share in range(out_ref.shape[0]):
        out_ref[share] = mixed[:, share * width : (share + 1) * width].astype(out_ref.dtype)


def route_kernel(got_ref, pick_ref, mix_ref):
    blocks, slots, length = pick_ref.shape
    targets = slots // SLOTS
    base = got_ref.shape[1] - targets - targets // 2
    iota = lambda shape, dim: lax.broadcasted_iota(jnp.int32, shape, dim)
    earlier = (iota((length, length), 0) > iota((length, length), 1)).astype(BF)
    earlier_t = (iota((length, length), 0) < iota((length, length), 1)).astype(BF)
    eye = (iota((length, length), 0) == iota((length, length), 1)).astype(BF)
    spread = (iota((targets, slots), 1) // SLOTS == iota((targets, slots), 0)).astype(BF)
    spread_t = (iota((slots, targets), 0) // SLOTS == iota((slots, targets), 1)).astype(BF)
    slot = (iota((length, slots), 1) % SLOTS).astype(F32)
    slot_t = (iota((slots, length), 0) % SLOTS).astype(F32)
    for block in range(blocks):
        first = got_ref[block, base : base + targets, :]
        last = got_ref[block, base + targets :, :]
        rest = length - DK
        last = jnp.concatenate([last[:, :rest], last[:, rest:]], axis=0)
        weight_t = jnp.concatenate([first, last], axis=1)
        named_t = weight_t.astype(F32) > 0.0
        weight = mm(eye, weight_t, NT)
        named = weight > 0.0
        place = jnp.where(named, mm(earlier, jnp.where(named, 1.0, 0.0)), -1.0)
        place_t = jnp.where(named_t, mm(jnp.where(named_t, 1.0, 0.0), earlier_t), -1.0)
        mix_ref[block] = jnp.where(mm(place, spread) == slot, mm(weight, spread), 0.0).astype(BF)
        pick_ref[block] = jnp.where(mm(spread_t, place_t) == slot_t, 1.0, 0.0).astype(BF)


def pick_kernel(pick_ref, token_ref, send_ref):
    targets = send_ref.shape[0]
    width = send_ref.shape[2]
    for block in range(pick_ref.shape[0]):
        rows = mm(pick_ref[block], token_ref[block]).astype(BF)
        send_ref[:, block * SLOTS : (block + 1) * SLOTS, :] = rows.reshape(targets, SLOTS, width)


def expert_kernel(rows_ref, gain_ref, gate_ref, up_ref, down_ref, out_ref, normed_ref):
    groups, shares, count, width = rows_ref.shape
    for group in range(groups):
        place = slice(group * count, (group + 1) * count)
        total = jnp.zeros((count, 1), F32)
        for share in range(shares):
            piece = rows_ref[group, share].astype(F32)
            total = total + jnp.sum(piece * piece, axis=1, keepdims=True)
        scaling = lax.rsqrt(total / (shares * width) + EPS)
        for share in range(shares):
            part = slice(share * width, (share + 1) * width)
            piece = rows_ref[group, share].astype(F32)
            normed_ref[place, part] = (piece * scaling * gain_ref[:, part]).astype(BF)
    normed = normed_ref[...]
    hidden = (silu(mm(normed, gate_ref[...])) * mm(normed, up_ref[...])).astype(BF)
    for share in range(shares):
        part = slice(share * width, (share + 1) * width)
        produced = mm(hidden, down_ref[:, part]).astype(BF)
        for group in range(groups):
            out_ref[group, share] = produced[group * count : (group + 1) * count]


def combine_kernel(mix_ref, rows_ref, out_ref):
    targets, _, width = rows_ref.shape
    for block in range(mix_ref.shape[0]):
        rows = rows_ref[:, block * SLOTS : (block + 1) * SLOTS, :].reshape(targets * SLOTS, width)
        out_ref[block] = mm(mix_ref[block], rows).astype(out_ref.dtype)


def swap(value, axes):
    return lax.all_to_all(value, axes, 0, 0, tiled=True)


def on_device(
    query_in,
    key_in,
    value_in,
    gate_in,
    decay_rate,
    beta_logit,
    head_gain,
    out_proj,
    residual_in,
    post_gain,
    expert_ids,
    route_weight,
    w_gate,
    w_up,
    w_down,
):
    length = query_in.shape[0]
    heads = decay_rate.shape[0]
    blocks = lax.axis_size("z")
    groups = lax.axis_size("x")
    shares = lax.axis_size("y") * lax.axis_size("c")
    share = lax.axis_index(("y", "c"))
    width = residual_in.shape[1] // shares
    count = blocks * SLOTS
    targets = groups * shares
    shape = jax.ShapeDtypeStruct

    rows = heads * DV // blocks
    packed = DK + rows + MARKS + targets + targets // 2
    send, inside, reach = call(
        mixer_kernel,
        (
            shape((blocks, packed, DK), BF),
            shape((heads, length, DV), F32),
            shape((heads, length, DK), BF),
        ),
        query_in,
        key_in,
        value_in,
        decay_rate,
        beta_logit,
        expert_ids.T,
        route_weight.T,
    )
    got = swap(send, "z")
    total = call(total_kernel, shape((DK + rows + MARKS, DK), BF), got)
    totals = swap(jnp.broadcast_to(total, (groups,) + total.shape), "x")
    pick, mix = call(
        route_kernel,
        (
            shape((blocks, targets * SLOTS, length), BF),
            shape((blocks, length, targets * SLOTS), BF),
        ),
        got,
    )
    enter = call(
        state_kernel,
        shape((blocks, rows, DK), BF),
        lax.axis_index("x").reshape(1),
        totals,
        got,
        in_specs=[pl.BlockSpec(memory_space=pltpu.SMEM)]
        + [pl.BlockSpec(memory_space=pltpu.VMEM)] * 2,
    )
    state = swap(enter, "z").reshape(heads, DV, DK)

    partial = call(
        output_kernel,
        shape((shares, length, width), BF),
        inside,
        reach,
        state,
        gate_in,
        head_gain.reshape(1, DV),
        out_proj,
    )
    mixed = jnp.sum(swap(partial, ("y", "c")).astype(F32), axis=0)
    residual = lax.dynamic_slice_in_dim(residual_in, share * width, width, 1)
    middle = (residual.astype(F32) + mixed).astype(BF)

    tokens = lax.all_gather(middle, "z")
    send = call(pick_kernel, shape((targets, count, width), BF), pick, tokens)
    arrived = swap(send, ("x", "y", "c")).reshape(groups, shares, count, width)
    produced = call(
        expert_kernel,
        shape((groups, shares, count, width), BF),
        arrived,
        post_gain.reshape(1, -1),
        w_gate[0],
        w_up[0],
        w_down[0],
        scratch_shapes=[pltpu.VMEM((groups * count, shares * width), BF)],
    )
    returned = swap(produced.reshape(targets, count, width), ("x", "y", "c"))
    mixes = call(combine_kernel, shape((blocks, length, width), BF), mix, returned)
    expert_mix = jnp.sum(swap(mixes, "z").astype(F32), axis=0)
    layer_out = (middle.astype(F32) + expert_mix).astype(BF)
    return (middle, layer_out)


def solution(mesh):
    ctx, exp = mesh.devices.shape
    split = Mesh(mesh.devices.reshape(4, ctx // 4, exp // 2, 2), ("x", "z", "y", "c"))
    row, col = ("x", "z"), ("y", "c")
    in_specs = (
        P(row, col),
        P(row, col),
        P(row, col),
        P(row, col),
        P(col, row),
        P(col, row),
        P(),
        P(col, None),
        P(row, None),
        P(),
        P(row, None),
        P(row, None),
        P(row + col, None, None),
        P(row + col, None, None),
        P(row + col, None, None),
    )
    out_specs = (P(row, col), P(row, col))
    return jax.shard_map(
        on_device, mesh=split, in_specs=in_specs, out_specs=out_specs, check_vma=False
    )
```

```python
import functools

import jax
import jax.numpy as jnp
from jax import lax
from jax.experimental import pallas as pl
from jax.experimental.pallas import tpu as pltpu
from jax.sharding import Mesh, PartitionSpec as P

DK = 128
DV = 128
SLOTS = 16
MARKS = 16
TARGETS = 32
SHARES = 8
EPS = 1e-06
BF = jnp.bfloat16
F32 = jnp.float32
NN = ((1,), (0,))
NT = ((1,), (1,))
TN = ((0,), (0,))
MIB = 1024 * 1024


def mm(left, right, dims=NN):
    return lax.dot_general(
        left.astype(BF), right.astype(BF), (dims, ((), ())), preferred_element_type=F32
    )


def exact(left, right, dims=NN):
    return lax.dot_general(
        left, right, (dims, ((), ())), precision=lax.Precision.HIGHEST, preferred_element_type=F32
    )


def halves(value):
    high = value.astype(BF)
    return high, (value - high.astype(F32)).astype(BF)


def mm3(left, right, dims=NN):
    left_high, left_low = halves(left)
    right_high, right_low = halves(right)
    return (
        mm(left_high, right_high, dims)
        + mm(left_high, right_low, dims)
        + mm(left_low, right_high, dims)
    )


def pieces(value):
    first, second = halves(value)
    third = (value - first.astype(F32) - second.astype(F32)).astype(BF)
    row = lax.broadcasted_iota(jnp.int32, value.shape, 0)
    return jnp.where(row == 0, first, jnp.where(row == 1, second, third))


def joined(marks):
    marks = marks.astype(F32)
    return marks[0:1] + marks[1:2] + marks[2:3]


def unpack(got, rows):
    fade = joined(got[DK + rows : DK + rows + MARKS, :])
    return got[:DK, :], got[DK : DK + rows, :].astype(F32), fade


def advance(state, removed, fade):
    high, low = halves(state)
    return fade * state - (mm(high, removed) + mm(low, removed))


def silu(value):
    return value / (1.0 + jnp.exp(-value))


def call(kernel, out_shape, *operands, vmem, flops=0, moved=0, **more):
    return pl.pallas_call(
        kernel,
        out_shape=out_shape,
        compiler_params=pltpu.CompilerParams(vmem_limit_bytes=vmem * MIB),
        cost_estimate=pl.CostEstimate(flops=flops, bytes_accessed=moved, transcendentals=0),
        **more,
    )(*operands)


def mixer_kernel(*refs):
    count = len(refs) // 2 - 2
    sources, (send_ref, inside_ref, reach_ref) = refs[:count], refs[count : count + 3]
    held, sems = refs[count + 3 : -1], refs[-1]
    copies = [
        pltpu.make_async_copy(source, target, sems.at[i])
        for i, (source, target) in enumerate(zip(sources, held))
    ]
    for copy in copies:
        copy.start()
    for copy in copies:
        copy.wait()
    q_ref, k_ref, v_ref, decay_ref, logit_ref, ids_ref, weight_ref = held
    length = q_ref.shape[0]
    heads = decay_ref.shape[0]
    ratio = heads // (q_ref.shape[1] // DK)
    places = send_ref.shape[0]
    cuts = places // heads
    rows = DV // cuts
    targets = TARGETS
    shares = SHARES
    row = lax.broadcasted_iota(jnp.int32, (length, length), 0)
    col = lax.broadcasted_iota(jnp.int32, (length, length), 1)
    on = row >= col
    below = row > col
    eye = jnp.where(row == col, 1.0, 0.0)
    tri = jnp.where(on, 1.0, 0.0)
    rate_row = 1.0 / (1.0 + jnp.exp(-logit_ref[...]))
    log_row = -exact(decay_ref[...], tri, NT)
    log_col = -exact(tri, decay_ref[...], NT)
    rate_col = exact(eye, rate_row, NT)
    ones = jnp.ones((8, DK), F32)
    systems, weights, scales = [], [], []
    for group in range(heads // ratio):
        part = slice(group * DK, (group + 1) * DK)
        query = q_ref[:, part]
        key = k_ref[:, part]
        query_f = query.astype(F32)
        key_f = key.astype(F32)
        query_scale = lax.rsqrt(jnp.sum(query_f * query_f, axis=1, keepdims=True) + EPS) * DK**-0.5
        key_scale = lax.rsqrt(jnp.sum(key_f * key_f, axis=1, keepdims=True) + EPS)
        key_scale_row = lax.rsqrt(exact(ones, key_f * key_f, NT)[:1] + EPS)
        key_key = mm(key, key, NT) * (key_scale * key_scale_row)
        query_key = mm(query, key, NT) * (query_scale * key_scale_row)
        for head in range(group * ratio, (group + 1) * ratio):
            apart = jnp.where(on, log_col[:, head : head + 1] - log_row[head : head + 1, :], 0.0)
            fading = jnp.where(on, jnp.exp(apart), 0.0) * rate_row[head : head + 1, :]
            systems.append(jnp.where(below, key_key * fading, 0.0))
            weights.append(query_key * fading)
            scales.append((query_f * query_scale, key_f * key_scale, key_scale, key))
    inverses = [eye - jnp.where(row // 2 == col // 2, system, 0.0) for system in systems]
    size = 2
    while size < length:
        lower = (row // (2 * size) == col // (2 * size)) & (row // size > col // size)
        crossing = [
            mm(jnp.where(lower, system, 0.0), inverse)
            for system, inverse in zip(systems, inverses)
        ]
        inverses = [
            inverse - mm(inverse, cross) for inverse, cross in zip(inverses, crossing)
        ]
        size *= 2
    for head in range(heads):
        query_n, key_n, key_scale, key = scales[head]
        lead = jnp.exp(log_col[:, head : head + 1])
        value = v_ref[:, head * DV : (head + 1) * DV].astype(F32)
        target = jnp.concatenate([value, lead * key_n], axis=1)
        solved = mm(inverses[head], target)
        missing = target - solved - mm3(systems[head], solved)
        solved = solved + mm(inverses[head], missing)
        both = mm3(weights[head], solved)
        inside_ref[head] = both[:, :DV]
        reach_ref[head] = (lead * query_n - both[:, DV:]).astype(reach_ref.dtype)
        last = log_col[length - 1 : length, head : head + 1]
        tail = jnp.exp(last - log_col[:, head : head + 1]) * rate_col[:, head : head + 1] * key_scale
        high, low = halves(solved * tail)
        written = mm(high, key, TN) + mm(low, key, TN)
        removed = written[DV:].astype(BF)
        added = written[:DV].astype(BF)
        fade = pieces(jnp.broadcast_to(jnp.exp(last), (MARKS, DK)))
        for cut in range(cuts):
            place = head * cuts + cut
            send_ref[place, :DK, :] = removed
            send_ref[place, DK : DK + rows, :] = added[cut * rows : (cut + 1) * rows]
            send_ref[place, DK + rows : DK + rows + MARKS, :] = fade
    base = DK + rows + MARKS
    number = lax.broadcasted_iota(jnp.int32, (targets, length), 0)
    number = (number // shares) * (places * shares) + number % shares
    for place in range(places):
        weight = jnp.zeros((targets, length), F32)
        for choice in range(ids_ref.shape[0]):
            hit = ids_ref[choice : choice + 1, :] == number + place * shares
            weight = weight + jnp.where(hit, weight_ref[choice : choice + 1, :], 0.0)
        weight = weight.astype(BF)
        send_ref[place, base : base + targets, :] = weight[:, :DK]
        send_ref[place, base + targets :, :] = jnp.concatenate(
            [weight[: targets // 2, DK:], weight[targets // 2 :, DK:]], axis=1
        )


def total_kernel(got_ref, total_ref):
    blocks = got_ref.shape[0]
    rows = total_ref.shape[0] - DK - MARKS
    row = lax.broadcasted_iota(jnp.int32, (DK, DK), 0)
    col = lax.broadcasted_iota(jnp.int32, (DK, DK), 1)
    eye = jnp.where(row == col, 1.0, 0.0)
    whole = jnp.ones((1, DK), F32)
    product = eye
    state = jnp.zeros((rows, DK), F32)
    for block in range(blocks):
        removed, added, fade = unpack(got_ref[block], rows)
        if block == 0:
            product = fade * eye - removed.astype(F32)
            state = added
        else:
            product = advance(product, removed, fade)
            state = advance(state, removed, fade) + added
        whole = whole * fade
    total_ref[:DK, :] = (whole * eye - product).astype(BF)
    total_ref[DK : DK + rows, :] = state.astype(BF)
    total_ref[DK + rows :, :] = pieces(jnp.broadcast_to(whole, (MARKS, DK)))


def state_kernel(here_ref, got_ref, *rest):
    totals, enter_ref = rest[:-1], rest[-1]
    blocks, rows, _ = enter_ref.shape
    state = jnp.zeros((rows, DK), F32)
    for distance in range(len(totals), 0, -1):
        removed, added, fade = unpack(totals[distance - 1], rows)
        state = jnp.where(distance <= here_ref[0], advance(state, removed, fade) + added, state)
    for block in range(blocks):
        enter_ref[block] = state.astype(BF)
        if block < blocks - 1:
            removed, added, fade = unpack(got_ref[block], rows)
            state = advance(state, removed, fade) + added


def output_kernel(
    here_ref, inside_ref, reach_ref, state_ref, gate_ref, gain_ref, proj_ref, keep_ref, give_ref
):
    heads = inside_ref.shape[0]
    gated = []
    for head in range(heads):
        part = slice(head * DV, (head + 1) * DV)
        output = inside_ref[head] + mm(reach_ref[head], state_ref[head], NT)
        scaling = lax.rsqrt(jnp.mean(output * output, axis=1, keepdims=True) + EPS)
        opened = silu(gate_ref[:, part].astype(F32))
        gated.append((output * scaling * gain_ref[...] * opened).astype(BF))
    gated = jnp.concatenate(gated, axis=1)
    columns, _, width = keep_ref.shape
    for distance in range(columns):
        column = lax.rem(here_ref[0] + distance, columns)
        for core, out_ref in ((here_ref[1], keep_ref), (1 - here_ref[1], give_ref)):
            first = pl.multiple_of((column * 2 + core) * width, width)
            mixed = mm(gated, proj_ref[:, pl.ds(first, width)])
            out_ref[distance] = mixed.astype(out_ref.dtype)


def route_kernel(here_ref, got_ref, pick_ref, mix_ref):
    blocks, slots, length = pick_ref.shape
    targets = slots // SLOTS
    base = got_ref.shape[1] - targets - targets // 2
    iota = lambda shape, dim: lax.broadcasted_iota(jnp.int32, shape, dim)
    earlier = (iota((length, length), 0) > iota((length, length), 1)).astype(BF)
    earlier_t = (iota((length, length), 0) < iota((length, length), 1)).astype(BF)
    eye = (iota((length, length), 0) == iota((length, length), 1)).astype(BF)
    spread = (iota((targets, slots), 1) // SLOTS == iota((targets, slots), 0)).astype(BF)
    spread_t = (iota((slots, targets), 0) // SLOTS == iota((slots, targets), 1)).astype(BF)
    slot = (iota((length, slots), 1) % SLOTS).astype(F32)
    slot_t = (iota((slots, length), 0) % SLOTS).astype(F32)
    for block in range(blocks):
        source = lax.rem(here_ref[0] + blocks - block, blocks)
        first = got_ref[source, base : base + targets, :]
        last = got_ref[source, base + targets :, :]
        rest = length - DK
        last = jnp.concatenate([last[:, :rest], last[:, rest:]], axis=0)
        weight_t = jnp.concatenate([first, last], axis=1)
        named_t = weight_t.astype(F32) > 0.0
        weight = mm(eye, weight_t, NT)
        named = weight > 0.0
        place = jnp.where(named, mm(earlier, jnp.where(named, 1.0, 0.0)), -1.0)
        place_t = jnp.where(named_t, mm(jnp.where(named_t, 1.0, 0.0), earlier_t), -1.0)
        mix_ref[block] = jnp.where(mm(place, spread) == slot, mm(weight, spread), 0.0).astype(BF)
        pick_ref[block] = jnp.where(mm(spread_t, place_t) == slot_t, 1.0, 0.0).astype(BF)


def pick_kernel(pick_ref, *rest):
    tokens, send_ref = rest[:-1], rest[-1]
    targets = send_ref.shape[0]
    width = send_ref.shape[2]
    for block in range(pick_ref.shape[0]):
        rows = mm(pick_ref[block], tokens[block][...]).astype(BF)
        send_ref[:, block * SLOTS : (block + 1) * SLOTS, :] = rows.reshape(targets, SLOTS, width)


def expert_kernel(rows_ref, gain_ref, gate_ref, up_ref, down_ref, out_ref, normed_ref):
    groups, shares, count, width = rows_ref.shape
    for group in range(groups):
        place = slice(group * count, (group + 1) * count)
        total = jnp.zeros((count, 1), F32)
        for share in range(shares):
            piece = rows_ref[group, share].astype(F32)
            total = total + jnp.sum(piece * piece, axis=1, keepdims=True)
        scaling = lax.rsqrt(total / (shares * width) + EPS)
        for share in range(shares):
            part = slice(share * width, (share + 1) * width)
            piece = rows_ref[group, share].astype(F32)
            normed_ref[place, part] = (piece * scaling * gain_ref[:, part]).astype(BF)
    normed = normed_ref[...]
    hidden = (silu(mm(normed, gate_ref[...])) * mm(normed, up_ref[...])).astype(BF)
    for share in range(shares):
        part = slice(share * width, (share + 1) * width)
        produced = mm(hidden, down_ref[:, part]).astype(BF)
        for group in range(groups):
            out_ref[group, share] = produced[group * count : (group + 1) * count]


def combine_kernel(mix_ref, rows_ref, *outs):
    targets, _, width = rows_ref.shape
    for block in range(mix_ref.shape[0]):
        rows = rows_ref[:, block * SLOTS : (block + 1) * SLOTS, :].reshape(targets * SLOTS, width)
        outs[block][...] = mm(mix_ref[block], rows).astype(outs[block].dtype)


SCALAR = pl.BlockSpec(memory_space=pltpu.SMEM)
VECTOR = pl.BlockSpec(memory_space=pltpu.VMEM)


def shifted(value, axis, distance):
    size = lax.axis_size(axis)
    return lax.ppermute(value, axis, [(i, (i + distance) % size) for i in range(size)])


def swap(value, axes):
    return lax.all_to_all(value, axes, 0, 0, tiled=True)


def on_device(
    query_in,
    key_in,
    value_in,
    gate_in,
    decay_rate,
    beta_logit,
    head_gain,
    out_proj,
    residual_in,
    post_gain,
    expert_ids,
    route_weight,
    w_gate,
    w_up,
    w_down,
):
    length = query_in.shape[0]
    heads = decay_rate.shape[0]
    blocks = lax.axis_size("z")
    groups = lax.axis_size("x")
    shares = lax.axis_size("y") * lax.axis_size("c")
    share = lax.axis_index(("y", "c"))
    width = residual_in.shape[1] // shares
    count = blocks * SLOTS
    targets = groups * shares
    shape = jax.ShapeDtypeStruct

    rows = heads * DV // blocks
    packed = DK + rows + MARKS + targets + targets // 2
    operands = (
        query_in,
        key_in,
        value_in,
        decay_rate,
        beta_logit,
        expert_ids.T,
        route_weight.T,
    )
    send, inside, reach = call(
        mixer_kernel,
        (
            shape((blocks, packed, DK), BF),
            shape((heads, length, DV), F32),
            shape((heads, length, DK), BF),
        ),
        *operands,
        vmem=24,
        in_specs=[pl.BlockSpec(memory_space=pl.ANY)] * len(operands),
        scratch_shapes=[pltpu.VMEM(item.shape, item.dtype) for item in operands]
        + [pltpu.SemaphoreType.DMA((len(operands),))],
    )
    got = swap(send, "z")
    total = call(total_kernel, shape((DK + rows + MARKS, DK), BF), got, vmem=8)
    totals = [shifted(total, "x", distance) for distance in range(1, groups)]
    pick, mix = call(
        route_kernel,
        (
            shape((blocks, targets * SLOTS, length), BF),
            shape((blocks, length, targets * SLOTS), BF),
        ),
        lax.axis_index("z").reshape(1),
        got,
        vmem=12,
        in_specs=[SCALAR, VECTOR],
    )
    enter = call(
        state_kernel,
        shape((blocks, rows, DK), BF),
        lax.axis_index("x").reshape(1),
        got,
        *totals,
        vmem=8,
        in_specs=[SCALAR] + [VECTOR] * (1 + len(totals)),
    )
    state = swap(enter, "z").reshape(heads, DV, DK)

    here = jnp.stack([lax.axis_index("y"), lax.axis_index("c")])
    columns = lax.axis_size("y")
    keep, give = call(
        output_kernel,
        (shape((columns, length, width), F32), shape((columns, length, width), BF)),
        here,
        inside,
        reach,
        state,
        gate_in,
        head_gain.reshape(1, DV),
        out_proj,
        vmem=16,
        in_specs=[SCALAR] + [VECTOR] * 6,
    )
    both = keep + shifted(give, "c", 1).astype(F32)
    mixed = both[0]
    for distance in range(1, columns):
        mixed = mixed + shifted(both[distance].astype(BF), "y", distance).astype(F32)
    residual = lax.dynamic_slice_in_dim(residual_in, share * width, width, 1)
    middle = (residual.astype(F32) + mixed).astype(BF)

    tokens = [middle] + [shifted(middle, "z", distance) for distance in range(1, blocks)]
    send = call(pick_kernel, shape((targets, count, width), BF), pick, *tokens, vmem=12)
    arrived = swap(send, ("x", "y", "c")).reshape(groups, shares, count, width)
    produced = call(
        expert_kernel,
        shape((groups, shares, count, width), BF),
        arrived,
        post_gain.reshape(1, -1),
        w_gate[0],
        w_up[0],
        w_down[0],
        vmem=24,
        scratch_shapes=[pltpu.VMEM((groups * count, shares * width), BF)],
    )
    returned = swap(produced.reshape(targets, count, width), ("x", "y", "c"))
    mixes = call(
        combine_kernel,
        (shape((length, width), F32),) + (shape((length, width), BF),) * (blocks - 1),
        mix,
        returned,
        vmem=16,
    )
    expert_mix = mixes[0]
    for distance in range(1, blocks):
        expert_mix = expert_mix + shifted(mixes[distance], "z", -distance).astype(F32)
    layer_out = (middle.astype(F32) + expert_mix).astype(BF)
    return (middle, layer_out)


def solution(mesh):
    ctx, exp = mesh.devices.shape
    split = Mesh(mesh.devices.reshape(4, ctx // 4, exp // 2, 2), ("x", "z", "y", "c"))
    row, col = ("x", "z"), ("y", "c")
    in_specs = (
        P(row, col),
        P(row, col),
        P(row, col),
        P(row, col),
        P(col, row),
        P(col, row),
        P(),
        P(col, None),
        P(row, None),
        P(),
        P(row, None),
        P(row, None),
        P(row + col, None, None),
        P(row + col, None, None),
        P(row + col, None, None),
    )
    out_specs = (P(row, col), P(row, col))
    return jax.shard_map(
        on_device, mesh=split, in_specs=in_specs, out_specs=out_specs, check_vma=False
    )
```

```python
import functools

import jax
import jax.numpy as jnp
from jax import lax
from jax.experimental import pallas as pl
from jax.experimental.pallas import tpu as pltpu
from jax.sharding import Mesh, PartitionSpec as P

DK = 128
DV = 128
SLOTS = 16
MARKS = 16
SHARES = 8
EPS = 1e-06
BF = jnp.bfloat16
F32 = jnp.float32
NN = ((1,), (0,))
NT = ((1,), (1,))
TN = ((0,), (0,))
MIB = 1024 * 1024


def mm(left, right, dims=NN):
    return lax.dot_general(
        left.astype(BF), right.astype(BF), (dims, ((), ())), preferred_element_type=F32
    )


def exact(left, right, dims=NN):
    return lax.dot_general(
        left, right, (dims, ((), ())), precision=lax.Precision.HIGHEST, preferred_element_type=F32
    )


def halves(value):
    high = value.astype(BF)
    return high, (value - high.astype(F32)).astype(BF)


def mm3(left, right, dims=NN):
    left_high, left_low = halves(left)
    right_high, right_low = halves(right)
    return (
        mm(left_high, right_high, dims)
        + mm(left_high, right_low, dims)
        + mm(left_low, right_high, dims)
    )


def pieces(value):
    first, second = halves(value)
    third = (value - first.astype(F32) - second.astype(F32)).astype(BF)
    row = lax.broadcasted_iota(jnp.int32, value.shape, 0)
    return jnp.where(row == 0, first, jnp.where(row == 1, second, third))


def joined(marks):
    marks = marks.astype(F32)
    return marks[0:1] + marks[1:2] + marks[2:3]


def unpack(got, rows):
    fade = joined(got[DK + rows : DK + rows + MARKS, :])
    return got[:DK, :], got[DK : DK + rows, :].astype(F32), fade


def advance(state, removed, fade):
    high, low = halves(state)
    return fade * state - (mm(high, removed) + mm(low, removed))


def silu(value):
    return value / (1.0 + jnp.exp(-value))


def call(kernel, out_shape, *operands, vmem, flops=0, moved=0, **more):
    return pl.pallas_call(
        kernel,
        out_shape=out_shape,
        compiler_params=pltpu.CompilerParams(vmem_limit_bytes=vmem * MIB),
        cost_estimate=pl.CostEstimate(flops=flops, bytes_accessed=moved, transcendentals=0),
        **more,
    )(*operands)


def brought(sources, held, sems):
    copies = [
        pltpu.make_async_copy(source, target, sems.at[i])
        for i, (source, target) in enumerate(zip(sources, held))
    ]
    for copy in copies:
        copy.start()
    for copy in copies:
        copy.wait()


def key_norms(key):
    key_f = key.astype(F32)
    square = key_f * key_f
    scale = lax.rsqrt(jnp.sum(square, axis=1, keepdims=True) + EPS)
    scale_row = lax.rsqrt(exact(jnp.ones((8, DK), F32), square, NT)[:1] + EPS)
    return scale, scale_row


def order(length):
    row = lax.broadcasted_iota(jnp.int32, (length, length), 0)
    col = lax.broadcasted_iota(jnp.int32, (length, length), 1)
    return row, col


def faded(on, log_col, log_row, rate_row):
    apart = jnp.where(on, log_col - log_row, 0.0)
    return jnp.where(on, jnp.exp(apart), 0.0) * rate_row


def logs(decay, on):
    tri = jnp.where(on, 1.0, 0.0)
    return -exact(decay, tri, NT), -exact(tri, decay, NT)


def solve_kernel(*refs):
    count = (len(refs) - 3) // 2
    sources, (send_ref, solved_ref) = refs[:count], refs[count : count + 2]
    held, sems = refs[count + 2 : -1], refs[-1]
    brought(sources, held, sems)
    k_ref, v_ref, decay_ref, logit_ref = held
    length = k_ref.shape[0]
    heads = decay_ref.shape[0]
    ratio = heads // (k_ref.shape[1] // DK)
    cuts = send_ref.shape[0] // heads
    rows = DV // cuts
    row, col = order(length)
    on = row >= col
    below = row > col
    eye = jnp.where(row == col, 1.0, 0.0)
    rate_row = 1.0 / (1.0 + jnp.exp(-logit_ref[...]))
    log_row, log_col = logs(decay_ref[...], on)
    rate_col = exact(eye, rate_row, NT)
    systems, keys = [], []
    for group in range(heads // ratio):
        key = k_ref[:, group * DK : (group + 1) * DK]
        scale, scale_row = key_norms(key)
        key_key = mm(key, key, NT) * (scale * scale_row)
        for head in range(group * ratio, (group + 1) * ratio):
            pick = slice(head, head + 1)
            fading = faded(on, log_col[:, pick], log_row[pick], rate_row[pick])
            systems.append(jnp.where(below, key_key * fading, 0.0))
            keys.append((key, scale))
    inverses = [eye - jnp.where(row // 2 == col // 2, system, 0.0) for system in systems]
    size = 2
    while size < length:
        lower = (row // (2 * size) == col // (2 * size)) & (row // size > col // size)
        crossing = [
            mm(jnp.where(lower, system, 0.0), inverse)
            for system, inverse in zip(systems, inverses)
        ]
        inverses = [
            inverse - mm(inverse, cross) for inverse, cross in zip(inverses, crossing)
        ]
        size *= 2
    targets = []
    for head in range(heads):
        key, scale = keys[head]
        lead = jnp.exp(log_col[:, head : head + 1])
        value = v_ref[:, head * DV : (head + 1) * DV].astype(F32)
        targets.append(jnp.concatenate([value, lead * scale * key.astype(F32)], axis=1))
    firsts = [mm(inverses[head], targets[head]) for head in range(heads)]
    missing = [
        targets[head] - firsts[head] - mm3(systems[head], firsts[head]) for head in range(heads)
    ]
    solutions = [firsts[head] + mm(inverses[head], missing[head]) for head in range(heads)]
    for head in range(heads):
        key, scale = keys[head]
        solved_ref[head] = solutions[head]
        last = log_col[length - 1 : length, head : head + 1]
        tail = jnp.exp(last - log_col[:, head : head + 1]) * rate_col[:, head : head + 1] * scale
        high, low = halves(solutions[head] * tail)
        written = mm(high, key, TN) + mm(low, key, TN)
        removed = written[DV:].astype(BF)
        added = written[:DV].astype(BF)
        fade = pieces(jnp.broadcast_to(jnp.exp(last), (MARKS, DK)))
        for cut in range(cuts):
            place = head * cuts + cut
            send_ref[place, :DK, :] = removed
            send_ref[place, DK : DK + rows, :] = added[cut * rows : (cut + 1) * rows]
            send_ref[place, DK + rows :, :] = fade


def inner_kernel(
    q_ref, k_ref, decay_ref, logit_ref, solved_ref, ids_ref, weight_ref, inside_ref, reach_ref, route_ref
):
    length = q_ref.shape[0]
    heads = decay_ref.shape[0]
    ratio = heads // (q_ref.shape[1] // DK)
    row, col = order(length)
    on = row >= col
    rate_row = 1.0 / (1.0 + jnp.exp(-logit_ref[...]))
    log_row, log_col = logs(decay_ref[...], on)
    for group in range(heads // ratio):
        part = slice(group * DK, (group + 1) * DK)
        query = q_ref[:, part]
        key = k_ref[:, part]
        query_f = query.astype(F32)
        query_scale = lax.rsqrt(jnp.sum(query_f * query_f, axis=1, keepdims=True) + EPS) * DK**-0.5
        _, scale_row = key_norms(key)
        query_key = mm(query, key, NT) * (query_scale * scale_row)
        for head in range(group * ratio, (group + 1) * ratio):
            pick = slice(head, head + 1)
            weight = query_key * faded(on, log_col[:, pick], log_row[pick], rate_row[pick])
            both = mm3(weight, solved_ref[head])
            inside_ref[head] = both[:, :DV]
            reach = jnp.exp(log_col[:, pick]) * query_scale * query_f - both[:, DV:]
            reach_ref[head] = reach.astype(BF)
    places, packed, _ = route_ref.shape
    targets = packed * 2 // 3
    number = lax.broadcasted_iota(jnp.int32, (targets, length), 0)
    number = (number // SHARES) * (places * SHARES) + number % SHARES
    for place in range(places):
        weight = jnp.zeros((targets, length), F32)
        for choice in range(ids_ref.shape[0]):
            hit = ids_ref[choice : choice + 1, :] == number + place * SHARES
            weight = weight + jnp.where(hit, weight_ref[choice : choice + 1, :], 0.0)
        weight = weight.astype(BF)
        route_ref[place, :targets, :] = weight[:, :DK]
        route_ref[place, targets:, :] = jnp.concatenate(
            [weight[: targets // 2, DK:], weight[targets // 2 :, DK:]], axis=1
        )


def total_kernel(got_ref, total_ref):
    blocks = got_ref.shape[0]
    rows = total_ref.shape[0] - DK - MARKS
    row = lax.broadcasted_iota(jnp.int32, (DK, DK), 0)
    col = lax.broadcasted_iota(jnp.int32, (DK, DK), 1)
    eye = jnp.where(row == col, 1.0, 0.0)
    whole = jnp.ones((1, DK), F32)
    product = eye
    state = jnp.zeros((rows, DK), F32)
    for block in range(blocks):
        removed, added, fade = unpack(got_ref[block], rows)
        if block == 0:
            product = fade * eye - removed.astype(F32)
            state = added
        else:
            product = advance(product, removed, fade)
            state = advance(state, removed, fade) + added
        whole = whole * fade
    total_ref[:DK, :] = (whole * eye - product).astype(BF)
    total_ref[DK : DK + rows, :] = state.astype(BF)
    total_ref[DK + rows :, :] = pieces(jnp.broadcast_to(whole, (MARKS, DK)))


def state_kernel(here_ref, got_ref, route_ref, *rest):
    totals, enter_ref = rest[:-1], rest[-1]
    blocks = enter_ref.shape[0]
    rows = enter_ref.shape[1] - route_ref.shape[1]
    enter_ref[:, rows:, :] = route_ref[...]
    state = jnp.zeros((rows, DK), F32)
    for distance in range(len(totals), 0, -1):
        removed, added, fade = unpack(totals[distance - 1], rows)
        state = jnp.where(distance <= here_ref[0], advance(state, removed, fade) + added, state)
    for block in range(blocks):
        enter_ref[block, :rows, :] = state.astype(BF)
        if block < blocks - 1:
            removed, added, fade = unpack(got_ref[block], rows)
            state = advance(state, removed, fade) + added


def output_kernel(
    here_ref, inside_ref, reach_ref, state_ref, gate_ref, gain_ref, proj_ref, keep_ref, give_ref
):
    heads = inside_ref.shape[0]
    gated = []
    for head in range(heads):
        part = slice(head * DV, (head + 1) * DV)
        cuts = state_ref.shape[0] // heads
        places = range(head * cuts, (head + 1) * cuts)
        state = jnp.concatenate([state_ref[place, : DV // cuts] for place in places], axis=0)
        output = inside_ref[head] + mm(reach_ref[head], state, NT)
        scaling = lax.rsqrt(jnp.mean(output * output, axis=1, keepdims=True) + EPS)
        opened = silu(gate_ref[:, part].astype(F32))
        gated.append((output * scaling * gain_ref[...] * opened).astype(BF))
    gated = jnp.concatenate(gated, axis=1)
    columns, _, width = keep_ref.shape
    for distance in range(columns):
        column = lax.rem(here_ref[0] + distance, columns)
        for core, out_ref in ((here_ref[1], keep_ref), (1 - here_ref[1], give_ref)):
            first = pl.multiple_of((column * 2 + core) * width, width)
            mixed = mm(gated, proj_ref[:, pl.ds(first, width)])
            out_ref[distance] = mixed.astype(out_ref.dtype)


def route_kernel(here_ref, got_ref, pick_ref, mix_ref):
    blocks, slots, length = pick_ref.shape
    targets = slots // SLOTS
    base = got_ref.shape[1] - targets - targets // 2
    iota = lambda shape, dim: lax.broadcasted_iota(jnp.int32, shape, dim)
    earlier = (iota((length, length), 0) > iota((length, length), 1)).astype(BF)
    earlier_t = (iota((length, length), 0) < iota((length, length), 1)).astype(BF)
    eye = (iota((length, length), 0) == iota((length, length), 1)).astype(BF)
    spread = (iota((targets, slots), 1) // SLOTS == iota((targets, slots), 0)).astype(BF)
    spread_t = (iota((slots, targets), 0) // SLOTS == iota((slots, targets), 1)).astype(BF)
    slot = (iota((length, slots), 1) % SLOTS).astype(F32)
    slot_t = (iota((slots, length), 0) % SLOTS).astype(F32)
    for block in range(blocks):
        source = lax.rem(here_ref[0] + blocks - block, blocks)
        first = got_ref[source, base : base + targets, :]
        last = got_ref[source, base + targets :, :]
        rest = length - DK
        last = jnp.concatenate([last[:, :rest], last[:, rest:]], axis=0)
        weight_t = jnp.concatenate([first, last], axis=1)
        named_t = weight_t.astype(F32) > 0.0
        weight = mm(eye, weight_t, NT)
        named = weight > 0.0
        place = jnp.where(named, mm(earlier, jnp.where(named, 1.0, 0.0)), -1.0)
        place_t = jnp.where(named_t, mm(jnp.where(named_t, 1.0, 0.0), earlier_t), -1.0)
        mix_ref[block] = jnp.where(mm(place, spread) == slot, mm(weight, spread), 0.0).astype(BF)
        pick_ref[block] = jnp.where(mm(spread_t, place_t) == slot_t, 1.0, 0.0).astype(BF)


def pick_kernel(pick_ref, *rest):
    tokens, send_ref = rest[:-1], rest[-1]
    targets = send_ref.shape[0]
    width = send_ref.shape[2]
    blocks = pick_ref.shape[0]
    far = blocks // 2
    for block in range(blocks):
        place = block if block <= far else block + 1
        token = tokens[place][...]
        if block == far:
            token = jnp.concatenate([token, tokens[place + 1][...]], axis=0)
        rows = mm(pick_ref[block], token).astype(BF)
        send_ref[:, block * SLOTS : (block + 1) * SLOTS, :] = rows.reshape(targets, SLOTS, width)


def expert_kernel(rows_ref, gain_ref, gate_ref, up_ref, down_ref, out_ref, normed_ref):
    groups, shares, count, width = rows_ref.shape
    for group in range(groups):
        place = slice(group * count, (group + 1) * count)
        total = jnp.zeros((count, 1), F32)
        for share in range(shares):
            piece = rows_ref[group, share].astype(F32)
            total = total + jnp.sum(piece * piece, axis=1, keepdims=True)
        scaling = lax.rsqrt(total / (shares * width) + EPS)
        for share in range(shares):
            part = slice(share * width, (share + 1) * width)
            piece = rows_ref[group, share].astype(F32)
            normed_ref[place, part] = (piece * scaling * gain_ref[:, part]).astype(BF)
    normed = normed_ref[...]
    hidden = (silu(mm(normed, gate_ref[...])) * mm(normed, up_ref[...])).astype(BF)
    for share in range(shares):
        part = slice(share * width, (share + 1) * width)
        produced = mm(hidden, down_ref[:, part]).astype(BF)
        for group in range(groups):
            out_ref[group, share] = produced[group * count : (group + 1) * count]


def combine_kernel(mix_ref, rows_ref, *outs):
    targets, _, width = rows_ref.shape
    for block in range(mix_ref.shape[0]):
        rows = rows_ref[:, block * SLOTS : (block + 1) * SLOTS, :].reshape(targets * SLOTS, width)
        outs[block][...] = mm(mix_ref[block], rows).astype(outs[block].dtype)


SCALAR = pl.BlockSpec(memory_space=pltpu.SMEM)
VECTOR = pl.BlockSpec(memory_space=pltpu.VMEM)


def shifted(value, axis, distance):
    size = lax.axis_size(axis)
    return lax.ppermute(value, axis, [(i, (i + distance) % size) for i in range(size)])


def swap(value, axes):
    return lax.all_to_all(value, axes, 0, 0, tiled=True)


def spread_out(value, axis):
    half = value.shape[0] // 2
    right = [value, shifted(value, axis, 1), shifted(value, axis, 2)]
    left = [shifted(value, axis, -1), shifted(value, axis, -2)]
    right.append(shifted(right[2], axis, 1))
    left.append(shifted(left[1], axis, -1))
    far = [shifted(right[2][:half], axis, 2), shifted(left[1][half:], axis, -2)]
    return right + far + left[::-1]


def gathered_sum(parts, axis):
    def passed(value, distance):
        return shifted(value.astype(BF), axis, distance).astype(F32)

    half = parts[4].shape[0] // 2
    first = passed(parts[4][:half], -2)
    last = passed(parts[4][half:], 2)
    left = parts[2] + passed(parts[3], -1)
    right = parts[6] + passed(parts[5], 1)
    left = jnp.concatenate([left[:half] + first, left[half:]], axis=0)
    right = jnp.concatenate([right[:half], right[half:] + last], axis=0)
    near = passed(parts[1], -1) + passed(parts[7], 1)
    return parts[0] + near + (passed(left, -2) + passed(right, 2))


def on_device(
    query_in,
    key_in,
    value_in,
    gate_in,
    decay_rate,
    beta_logit,
    head_gain,
    out_proj,
    residual_in,
    post_gain,
    expert_ids,
    route_weight,
    w_gate,
    w_up,
    w_down,
):
    length = query_in.shape[0]
    heads = decay_rate.shape[0]
    blocks = lax.axis_size("z")
    groups = lax.axis_size("x")
    shares = lax.axis_size("y") * lax.axis_size("c")
    share = lax.axis_index(("y", "c"))
    width = residual_in.shape[1] // shares
    count = blocks * SLOTS
    targets = groups * shares
    shape = jax.ShapeDtypeStruct

    rows = heads * DV // blocks
    extra = targets + targets // 2
    operands = (key_in, value_in, decay_rate, beta_logit)
    send, solved = call(
        solve_kernel,
        (
            shape((blocks, DK + rows + MARKS, DK), BF),
            shape((heads, length, DV + DK), F32),
        ),
        *operands,
        vmem=24,
        in_specs=[pl.BlockSpec(memory_space=pltpu.HBM)] * len(operands),
        scratch_shapes=[pltpu.VMEM(item.shape, item.dtype) for item in operands]
        + [pltpu.SemaphoreType.DMA((len(operands),))],
    )
    got = swap(send, "z")
    inside, reach, route = call(
        inner_kernel,
        (
            shape((heads, length, DV), F32),
            shape((heads, length, DK), BF),
            shape((blocks, extra, DK), BF),
        ),
        query_in,
        key_in,
        decay_rate,
        beta_logit,
        solved,
        expert_ids.T,
        route_weight.T,
        vmem=16,
        flops=2 * 10**9,
        moved=3 * 10**6,
    )
    total = call(total_kernel, shape((DK + rows + MARKS, DK), BF), got, vmem=8)
    totals = [shifted(total, "x", distance) for distance in range(1, groups)]
    enter = call(
        state_kernel,
        shape((blocks, rows + extra, DK), BF),
        lax.axis_index("x").reshape(1),
        got,
        route,
        *totals,
        vmem=8,
        in_specs=[SCALAR] + [VECTOR] * (2 + len(totals)),
    )
    back = swap(enter, "z")
    pick, mix = call(
        route_kernel,
        (
            shape((blocks, targets * SLOTS, length), BF),
            shape((blocks, length, targets * SLOTS), BF),
        ),
        lax.axis_index("z").reshape(1),
        back,
        vmem=12,
        flops=10**9,
        moved=4 * 10**6,
        in_specs=[SCALAR, VECTOR],
    )

    here = jnp.stack([lax.axis_index("y"), lax.axis_index("c")])
    columns = lax.axis_size("y")
    keep, give = call(
        output_kernel,
        (shape((columns, length, width), F32), shape((columns, length, width), BF)),
        here,
        inside,
        reach,
        back,
        gate_in,
        head_gain.reshape(1, DV),
        out_proj,
        vmem=16,
        in_specs=[SCALAR] + [VECTOR] * 6,
    )
    both = keep + shifted(give, "c", 1).astype(F32)
    mixed = both[0]
    for distance in range(1, columns):
        mixed = mixed + shifted(both[distance].astype(BF), "y", distance).astype(F32)
    residual = lax.dynamic_slice_in_dim(residual_in, share * width, width, 1)
    middle = (residual.astype(F32) + mixed).astype(BF)

    tokens = spread_out(middle, "z")
    send = call(pick_kernel, shape((targets, count, width), BF), pick, *tokens, vmem=12)
    arrived = swap(send, ("x", "y", "c")).reshape(groups, shares, count, width)
    produced = call(
        expert_kernel,
        shape((groups, shares, count, width), BF),
        arrived,
        post_gain.reshape(1, -1),
        w_gate[0],
        w_up[0],
        w_down[0],
        vmem=24,
        scratch_shapes=[pltpu.VMEM((groups * count, shares * width), BF)],
    )
    returned = swap(produced.reshape(targets, count, width), ("x", "y", "c"))
    mixes = call(
        combine_kernel,
        tuple(shape((length, width), F32 if i in (0, 2, 6) else BF) for i in range(blocks)),
        mix,
        returned,
        vmem=16,
    )
    expert_mix = gathered_sum(mixes, "z")
    layer_out = (middle.astype(F32) + expert_mix).astype(BF)
    return (middle, layer_out)


def solution(mesh):
    ctx, exp = mesh.devices.shape
    split = Mesh(mesh.devices.reshape(4, ctx // 4, exp // 2, 2), ("x", "z", "y", "c"))
    row, col = ("x", "z"), ("y", "c")
    in_specs = (
        P(row, col),
        P(row, col),
        P(row, col),
        P(row, col),
        P(col, row),
        P(col, row),
        P(),
        P(col, None),
        P(row, None),
        P(),
        P(row, None),
        P(row, None),
        P(row + col, None, None),
        P(row + col, None, None),
        P(row + col, None, None),
    )
    out_specs = (P(row, col), P(row, col))
    return jax.shard_map(
        on_device, mesh=split, in_specs=in_specs, out_specs=out_specs, check_vma=False
    )
```

```python
import functools

import jax
import jax.numpy as jnp
from jax import lax
from jax.experimental import pallas as pl
from jax.experimental.pallas import tpu as pltpu
from jax.sharding import Mesh, PartitionSpec as P

DK = 128
DV = 128
SLOTS = 16
MARKS = 16
SHARES = 8
EPS = 1e-06
BF = jnp.bfloat16
F32 = jnp.float32
NN = ((1,), (0,))
NT = ((1,), (1,))
TN = ((0,), (0,))
MIB = 1024 * 1024


def mm(left, right, dims=NN):
    return lax.dot_general(
        left.astype(BF), right.astype(BF), (dims, ((), ())), preferred_element_type=F32
    )


def exact(left, right, dims=NN):
    return lax.dot_general(
        left, right, (dims, ((), ())), precision=lax.Precision.HIGHEST, preferred_element_type=F32
    )


def halves(value):
    high = value.astype(BF)
    return high, (value - high.astype(F32)).astype(BF)


def mm3(left, right, dims=NN):
    left_high, left_low = halves(left)
    right_high, right_low = halves(right)
    return (
        mm(left_high, right_high, dims)
        + mm(left_high, right_low, dims)
        + mm(left_low, right_high, dims)
    )


def pieces(value):
    first, second = halves(value)
    third = (value - first.astype(F32) - second.astype(F32)).astype(BF)
    row = lax.broadcasted_iota(jnp.int32, value.shape, 0)
    return jnp.where(row == 0, first, jnp.where(row == 1, second, third))


def joined(marks):
    marks = marks.astype(F32)
    return marks[0:1] + marks[1:2] + marks[2:3]


def unpack(got, rows):
    fade = joined(got[DK + rows : DK + rows + MARKS, :])
    return got[:DK, :], got[DK : DK + rows, :].astype(F32), fade


def advance(state, removed, fade):
    high, low = halves(state)
    return fade * state - (mm(high, removed) + mm(low, removed))


def silu(value):
    return value / (1.0 + jnp.exp(-value))


def call(kernel, out_shape, *operands, vmem, flops=0, moved=0, **more):
    return pl.pallas_call(
        kernel,
        out_shape=out_shape,
        compiler_params=pltpu.CompilerParams(vmem_limit_bytes=vmem * MIB),
        cost_estimate=pl.CostEstimate(flops=flops, bytes_accessed=moved, transcendentals=0),
        **more,
    )(*operands)


def brought(sources, held, sems):
    copies = [
        pltpu.make_async_copy(source, target, sems.at[i])
        for i, (source, target) in enumerate(zip(sources, held))
    ]
    for copy in copies:
        copy.start()
    for copy in copies:
        copy.wait()


def key_norms(key):
    key_f = key.astype(F32)
    square = key_f * key_f
    scale = lax.rsqrt(jnp.sum(square, axis=1, keepdims=True) + EPS)
    scale_row = lax.rsqrt(exact(jnp.ones((8, DK), F32), square, NT)[:1] + EPS)
    return scale, scale_row


def order(length):
    row = lax.broadcasted_iota(jnp.int32, (length, length), 0)
    col = lax.broadcasted_iota(jnp.int32, (length, length), 1)
    return row, col


def faded(on, log_col, log_row, rate_row):
    apart = jnp.where(on, log_col - log_row, 0.0)
    return jnp.where(on, jnp.exp(apart), 0.0) * rate_row


def logs(decay, on):
    tri = jnp.where(on, 1.0, 0.0)
    return -exact(decay, tri, NT), -exact(tri, decay, NT)


def solve_kernel(*refs):
    count = (len(refs) - 3) // 2
    sources, (send_ref, solved_ref) = refs[:count], refs[count : count + 2]
    held, sems = refs[count + 2 : -1], refs[-1]
    brought(sources, held, sems)
    k_ref, v_ref, decay_ref, logit_ref = held
    length = k_ref.shape[0]
    heads = decay_ref.shape[0]
    ratio = heads // (k_ref.shape[1] // DK)
    cuts = send_ref.shape[0] // heads
    rows = DV // cuts
    row, col = order(length)
    on = row >= col
    below = row > col
    eye = jnp.where(row == col, 1.0, 0.0)
    rate_row = 1.0 / (1.0 + jnp.exp(-logit_ref[...]))
    log_row, log_col = logs(decay_ref[...], on)
    rate_col = exact(eye, rate_row, NT)
    systems, keys = [], []
    for group in range(heads // ratio):
        key = k_ref[:, group * DK : (group + 1) * DK]
        scale, scale_row = key_norms(key)
        key_key = mm(key, key, NT) * (scale * scale_row)
        for head in range(group * ratio, (group + 1) * ratio):
            pick = slice(head, head + 1)
            fading = faded(on, log_col[:, pick], log_row[pick], rate_row[pick])
            systems.append(jnp.where(below, key_key * fading, 0.0))
            keys.append((key, scale))
    inverses = [eye - jnp.where(row // 2 == col // 2, system, 0.0) for system in systems]
    size = 2
    while size < length:
        lower = (row // (2 * size) == col // (2 * size)) & (row // size > col // size)
        crossing = [
            mm(jnp.where(lower, system, 0.0), inverse)
            for system, inverse in zip(systems, inverses)
        ]
        inverses = [
            inverse - mm(inverse, cross) for inverse, cross in zip(inverses, crossing)
        ]
        size *= 2
    targets = []
    for head in range(heads):
        key, scale = keys[head]
        lead = jnp.exp(log_col[:, head : head + 1])
        value = v_ref[:, head * DV : (head + 1) * DV].astype(F32)
        targets.append(jnp.concatenate([value, lead * scale * key.astype(F32)], axis=1))
    firsts = [mm(inverses[head], targets[head]) for head in range(heads)]
    missing = [
        targets[head] - firsts[head] - mm3(systems[head], firsts[head]) for head in range(heads)
    ]
    solutions = [firsts[head] + mm(inverses[head], missing[head]) for head in range(heads)]
    for head in range(heads):
        key, scale = keys[head]
        solved_ref[head] = solutions[head]
        last = log_col[length - 1 : length, head : head + 1]
        tail = jnp.exp(last - log_col[:, head : head + 1]) * rate_col[:, head : head + 1] * scale
        high, low = halves(solutions[head] * tail)
        written = mm(high, key, TN) + mm(low, key, TN)
        removed = written[DV:].astype(BF)
        added = written[:DV].astype(BF)
        fade = pieces(jnp.broadcast_to(jnp.exp(last), (MARKS, DK)))
        for cut in range(cuts):
            place = head * cuts + cut
            send_ref[place, :DK, :] = removed
            send_ref[place, DK : DK + rows, :] = added[cut * rows : (cut + 1) * rows]
            send_ref[place, DK + rows :, :] = fade


def inner_kernel(
    q_ref, k_ref, decay_ref, logit_ref, solved_ref, ids_ref, weight_ref, inside_ref, reach_ref, route_ref
):
    length = q_ref.shape[0]
    heads = decay_ref.shape[0]
    ratio = heads // (q_ref.shape[1] // DK)
    row, col = order(length)
    on = row >= col
    rate_row = 1.0 / (1.0 + jnp.exp(-logit_ref[...]))
    log_row, log_col = logs(decay_ref[...], on)
    for group in range(heads // ratio):
        part = slice(group * DK, (group + 1) * DK)
        query = q_ref[:, part]
        key = k_ref[:, part]
        query_f = query.astype(F32)
        query_scale = lax.rsqrt(jnp.sum(query_f * query_f, axis=1, keepdims=True) + EPS) * DK**-0.5
        _, scale_row = key_norms(key)
        query_key = mm(query, key, NT) * (query_scale * scale_row)
        for head in range(group * ratio, (group + 1) * ratio):
            pick = slice(head, head + 1)
            weight = query_key * faded(on, log_col[:, pick], log_row[pick], rate_row[pick])
            both = mm3(weight, solved_ref[head])
            inside_ref[head] = both[:, :DV]
            reach = jnp.exp(log_col[:, pick]) * query_scale * query_f - both[:, DV:]
            reach_ref[head] = reach.astype(BF)
    places, packed, _ = route_ref.shape
    targets = packed * 2 // 3
    number = lax.broadcasted_iota(jnp.int32, (targets, length), 0)
    number = (number // SHARES) * (places * SHARES) + number % SHARES
    for place in range(places):
        weight = jnp.zeros((targets, length), F32)
        for choice in range(ids_ref.shape[0]):
            hit = ids_ref[choice : choice + 1, :] == number + place * SHARES
            weight = weight + jnp.where(hit, weight_ref[choice : choice + 1, :], 0.0)
        weight = weight.astype(BF)
        route_ref[place, :targets, :] = weight[:, :DK]
        route_ref[place, targets:, :] = jnp.concatenate(
            [weight[: targets // 2, DK:], weight[targets // 2 :, DK:]], axis=1
        )


def total_kernel(got_ref, after_ref, total_ref):
    del after_ref
    blocks = got_ref.shape[0]
    rows = total_ref.shape[0] - DK - MARKS
    row = lax.broadcasted_iota(jnp.int32, (DK, DK), 0)
    col = lax.broadcasted_iota(jnp.int32, (DK, DK), 1)
    eye = jnp.where(row == col, 1.0, 0.0)
    whole = jnp.ones((1, DK), F32)
    product = eye
    state = jnp.zeros((rows, DK), F32)
    for block in range(blocks):
        removed, added, fade = unpack(got_ref[block], rows)
        if block == 0:
            product = fade * eye - removed.astype(F32)
            state = added
        else:
            product = advance(product, removed, fade)
            state = advance(state, removed, fade) + added
        whole = whole * fade
    total_ref[:DK, :] = (whole * eye - product).astype(BF)
    total_ref[DK : DK + rows, :] = state.astype(BF)
    total_ref[DK + rows :, :] = pieces(jnp.broadcast_to(whole, (MARKS, DK)))


def state_kernel(here_ref, got_ref, route_ref, *rest):
    totals, enter_ref = rest[:-1], rest[-1]
    blocks = enter_ref.shape[0]
    rows = enter_ref.shape[1] - route_ref.shape[1]
    enter_ref[:, rows:, :] = route_ref[...]
    state = jnp.zeros((rows, DK), F32)
    for distance in range(len(totals), 0, -1):
        removed, added, fade = unpack(totals[distance - 1], rows)
        state = jnp.where(distance <= here_ref[0], advance(state, removed, fade) + added, state)
    for block in range(blocks):
        enter_ref[block, :rows, :] = state.astype(BF)
        if block < blocks - 1:
            removed, added, fade = unpack(got_ref[block], rows)
            state = advance(state, removed, fade) + added


def output_kernel(
    here_ref, inside_ref, reach_ref, state_ref, gate_ref, gain_ref, proj_ref, rest_ref, keep_ref, give_ref
):
    heads = inside_ref.shape[0]
    gated = []
    for head in range(heads):
        part = slice(head * DV, (head + 1) * DV)
        cuts = state_ref.shape[0] // heads
        places = range(head * cuts, (head + 1) * cuts)
        state = jnp.concatenate([state_ref[place, : DV // cuts] for place in places], axis=0)
        output = inside_ref[head] + mm(reach_ref[head], state, NT)
        scaling = lax.rsqrt(jnp.mean(output * output, axis=1, keepdims=True) + EPS)
        opened = silu(gate_ref[:, part].astype(F32))
        gated.append((output * scaling * gain_ref[...] * opened).astype(BF))
    gated = jnp.concatenate(gated, axis=1)
    columns, _, width = keep_ref.shape
    for distance in range(columns):
        column = lax.rem(here_ref[2] + distance, columns)
        for core, out_ref in ((here_ref[3], keep_ref), (1 - here_ref[3], give_ref)):
            first = pl.multiple_of((column * 2 + core) * width, width)
            mixed = mm(gated, proj_ref[:, pl.ds(first, width)])
            if distance == 0 and out_ref is keep_ref:
                mixed = mixed + rest_ref[:, pl.ds(first, width)].astype(F32)
            out_ref[distance] = mixed.astype(out_ref.dtype)


def route_kernel(here_ref, got_ref, pick_ref, mix_ref):
    blocks, slots, length = pick_ref.shape
    targets = slots // SLOTS
    base = got_ref.shape[1] - targets - targets // 2
    iota = lambda shape, dim: lax.broadcasted_iota(jnp.int32, shape, dim)
    earlier = (iota((length, length), 0) > iota((length, length), 1)).astype(BF)
    earlier_t = (iota((length, length), 0) < iota((length, length), 1)).astype(BF)
    eye = (iota((length, length), 0) == iota((length, length), 1)).astype(BF)
    spread = (iota((targets, slots), 1) // SLOTS == iota((targets, slots), 0)).astype(BF)
    spread_t = (iota((slots, targets), 0) // SLOTS == iota((slots, targets), 1)).astype(BF)
    slot = (iota((length, slots), 1) % SLOTS).astype(F32)
    slot_t = (iota((slots, length), 0) % SLOTS).astype(F32)
    for block in range(blocks):
        source = lax.rem(here_ref[1] + blocks - block, blocks)
        first = got_ref[source, base : base + targets, :]
        last = got_ref[source, base + targets :, :]
        rest = length - DK
        last = jnp.concatenate([last[:, :rest], last[:, rest:]], axis=0)
        weight_t = jnp.concatenate([first, last], axis=1)
        named_t = weight_t.astype(F32) > 0.0
        weight = mm(eye, weight_t, NT)
        named = weight > 0.0
        place = jnp.where(named, mm(earlier, jnp.where(named, 1.0, 0.0)), -1.0)
        place_t = jnp.where(named_t, mm(jnp.where(named_t, 1.0, 0.0), earlier_t), -1.0)
        mix_ref[block] = jnp.where(mm(place, spread) == slot, mm(weight, spread), 0.0).astype(BF)
        pick_ref[block] = jnp.where(mm(spread_t, place_t) == slot_t, 1.0, 0.0).astype(BF)


def pick_kernel(pick_ref, *rest):
    tokens, send_ref = rest[:-1], rest[-1]
    targets = send_ref.shape[0]
    width = send_ref.shape[2]
    for block in range(pick_ref.shape[0]):
        rows = mm(pick_ref[block], tokens[block][...]).astype(BF)
        send_ref[:, block * SLOTS : (block + 1) * SLOTS, :] = rows.reshape(targets, SLOTS, width)


def expert_kernel(rows_ref, gain_ref, gate_ref, up_ref, down_ref, out_ref, normed_ref):
    groups, shares, count, width = rows_ref.shape
    for group in range(groups):
        place = slice(group * count, (group + 1) * count)
        total = jnp.zeros((count, 1), F32)
        for share in range(shares):
            piece = rows_ref[group, share].astype(F32)
            total = total + jnp.sum(piece * piece, axis=1, keepdims=True)
        scaling = lax.rsqrt(total / (shares * width) + EPS)
        for share in range(shares):
            part = slice(share * width, (share + 1) * width)
            piece = rows_ref[group, share].astype(F32)
            normed_ref[place, part] = (piece * scaling * gain_ref[:, part]).astype(BF)
    normed = normed_ref[...]
    hidden = (silu(mm(normed, gate_ref[...])) * mm(normed, up_ref[...])).astype(BF)
    for share in range(shares):
        part = slice(share * width, (share + 1) * width)
        produced = mm(hidden, down_ref[:, part]).astype(BF)
        for group in range(groups):
            out_ref[group, share] = produced[group * count : (group + 1) * count]


def combine_kernel(mix_ref, rows_ref, *outs):
    targets, _, width = rows_ref.shape
    for block in range(mix_ref.shape[0]):
        rows = rows_ref[:, block * SLOTS : (block + 1) * SLOTS, :].reshape(targets * SLOTS, width)
        outs[block][...] = mm(mix_ref[block], rows).astype(outs[block].dtype)


SCALAR = pl.BlockSpec(memory_space=pltpu.SMEM)
VECTOR = pl.BlockSpec(memory_space=pltpu.VMEM)
UNREAD = pl.BlockSpec(memory_space=pl.ANY)
REMOTE = pl.BlockSpec(memory_space=pltpu.HBM)


def shifted(value, axis, distance):
    size = lax.axis_size(axis)
    return lax.ppermute(value, axis, [(i, (i + distance) % size) for i in range(size)])


def swap(value, axes):
    return lax.all_to_all(value, axes, 0, 0, tiled=True)


def spread_out(value, axis):
    right = [value, shifted(value, axis, 1), shifted(value, axis, 2)]
    left = [shifted(value, axis, -1), shifted(value, axis, -2)]
    right.append(shifted(right[2], axis, 1))
    left.append(shifted(left[1], axis, -1))
    right.append(shifted(right[2], axis, 2))
    return right + left[::-1]


def gathered_sum(parts, axis):
    def passed(value, distance):
        return shifted(value.astype(BF), axis, distance).astype(F32)

    left = parts[2] + passed(parts[3], -1) + passed(parts[4], -2)
    right = parts[6] + passed(parts[5], 1)
    near = passed(parts[1], -1) + passed(parts[7], 1)
    return parts[0] + near + (passed(left, -2) + passed(right, 2))


def on_device(
    query_in,
    key_in,
    value_in,
    gate_in,
    decay_rate,
    beta_logit,
    head_gain,
    out_proj,
    residual_in,
    post_gain,
    expert_ids,
    route_weight,
    w_gate,
    w_up,
    w_down,
):
    length = query_in.shape[0]
    heads = decay_rate.shape[0]
    blocks = lax.axis_size("z")
    groups = lax.axis_size("x")
    shares = lax.axis_size("y") * lax.axis_size("c")
    width = residual_in.shape[1] // shares
    count = blocks * SLOTS
    targets = groups * shares
    shape = jax.ShapeDtypeStruct

    rows = heads * DV // blocks
    extra = targets + targets // 2
    here = jnp.stack([lax.axis_index(axis) for axis in ("x", "z", "y", "c")])
    operands = (key_in, value_in, decay_rate, beta_logit)
    send, solved = call(
        solve_kernel,
        (
            shape((blocks, DK + rows + MARKS, DK), BF),
            shape((heads, length, DV + DK), F32),
        ),
        *operands,
        vmem=62,
        in_specs=[REMOTE] * len(operands),
        scratch_shapes=[pltpu.VMEM(item.shape, item.dtype) for item in operands]
        + [pltpu.SemaphoreType.DMA((len(operands),))],
    )
    got = swap(send, "z")
    inside, reach, route = call(
        inner_kernel,
        (
            shape((heads, length, DV), F32),
            shape((heads, length, DK), BF),
            shape((blocks, extra, DK), BF),
        ),
        query_in,
        key_in,
        decay_rate,
        beta_logit,
        solved,
        expert_ids.T,
        route_weight.T,
        vmem=16,
        flops=2 * 10**9,
        moved=3 * 10**6,
    )
    total = call(
        total_kernel,
        shape((DK + rows + MARKS, DK), BF),
        got,
        route,
        vmem=8,
        in_specs=[VECTOR, UNREAD],
    )
    totals = [shifted(total, "x", distance) for distance in range(1, groups)]
    enter = call(
        state_kernel,
        shape((blocks, rows + extra, DK), BF),
        here,
        got,
        route,
        *totals,
        vmem=8,
        in_specs=[SCALAR] + [VECTOR] * (2 + len(totals)),
    )
    back = swap(enter, "z")
    pick, mix = call(
        route_kernel,
        (
            shape((blocks, targets * SLOTS, length), BF),
            shape((blocks, length, targets * SLOTS), BF),
        ),
        here,
        back,
        vmem=12,
        flops=10**9,
        moved=4 * 10**6,
        in_specs=[SCALAR, VECTOR],
    )

    columns = lax.axis_size("y")
    keep, give = call(
        output_kernel,
        (shape((columns, length, width), F32), shape((columns, length, width), BF)),
        here,
        inside,
        reach,
        back,
        gate_in,
        head_gain.reshape(1, DV),
        out_proj,
        residual_in,
        vmem=16,
        in_specs=[SCALAR] + [VECTOR] * 7,
    )
    both = keep + shifted(give, "c", 1).astype(F32)
    mixed = both[0]
    for distance in range(1, columns):
        mixed = mixed + shifted(both[distance].astype(BF), "y", distance).astype(F32)
    middle = mixed.astype(BF)

    tokens = spread_out(middle, "z")
    send = call(pick_kernel, shape((targets, count, width), BF), pick, *tokens, vmem=12)
    arrived = swap(send, ("x", "y", "c")).reshape(groups, shares, count, width)
    produced = call(
        expert_kernel,
        shape((groups, shares, count, width), BF),
        arrived,
        post_gain.reshape(1, -1),
        w_gate[0],
        w_up[0],
        w_down[0],
        vmem=24,
        scratch_shapes=[pltpu.VMEM((groups * count, shares * width), BF)],
    )
    returned = swap(produced.reshape(targets, count, width), ("x", "y", "c"))
    mixes = call(
        combine_kernel,
        tuple(shape((length, width), F32 if i in (0, 2, 6) else BF) for i in range(blocks)),
        mix,
        returned,
        vmem=16,
    )
    expert_mix = gathered_sum(mixes, "z")
    layer_out = (middle.astype(F32) + expert_mix).astype(BF)
    return (middle, layer_out)


def solution(mesh):
    ctx, exp = mesh.devices.shape
    split = Mesh(mesh.devices.reshape(4, ctx // 4, exp // 2, 2), ("x", "z", "y", "c"))
    row, col = ("x", "z"), ("y", "c")
    in_specs = (
        P(row, col),
        P(row, col),
        P(row, col),
        P(row, col),
        P(col, row),
        P(col, row),
        P(),
        P(col, None),
        P(row, None),
        P(),
        P(row, None),
        P(row, None),
        P(row + col, None, None),
        P(row + col, None, None),
        P(row + col, None, None),
    )
    out_specs = (P(row, col), P(row, col))
    return jax.shard_map(
        on_device, mesh=split, in_specs=in_specs, out_specs=out_specs, check_vma=False
    )
```

```python
import functools

import jax
import jax.numpy as jnp
from jax import lax
from jax.experimental import pallas as pl
from jax.experimental.pallas import tpu as pltpu
from jax.sharding import Mesh, PartitionSpec as P

DK = 128
DV = 128
SLOTS = 16
MARKS = 16
SHARES = 8
EPS = 1e-06
BF = jnp.bfloat16
F32 = jnp.float32
NN = ((1,), (0,))
NT = ((1,), (1,))
TN = ((0,), (0,))
MIB = 1024 * 1024


def mm(left, right, dims=NN):
    return lax.dot_general(
        left.astype(BF), right.astype(BF), (dims, ((), ())), preferred_element_type=F32
    )


def exact(left, right, dims=NN):
    return lax.dot_general(
        left, right, (dims, ((), ())), precision=lax.Precision.HIGHEST, preferred_element_type=F32
    )


def halves(value):
    high = value.astype(BF)
    return high, (value - high.astype(F32)).astype(BF)


def mm3(left, right, dims=NN):
    left_high, left_low = halves(left)
    right_high, right_low = halves(right)
    return (
        mm(left_high, right_high, dims)
        + mm(left_high, right_low, dims)
        + mm(left_low, right_high, dims)
    )


def pieces(value):
    first, second = halves(value)
    third = (value - first.astype(F32) - second.astype(F32)).astype(BF)
    row = lax.broadcasted_iota(jnp.int32, value.shape, 0)
    return jnp.where(row == 0, first, jnp.where(row == 1, second, third))


def joined(marks):
    marks = marks.astype(F32)
    return marks[0:1] + marks[1:2] + marks[2:3]


def unpack(got, rows):
    fade = joined(got[DK + rows : DK + rows + MARKS, :])
    return got[:DK, :], got[DK : DK + rows, :].astype(F32), fade


def advance(state, removed, fade):
    high, low = halves(state)
    return fade * state - (mm(high, removed) + mm(low, removed))


def silu(value):
    return value / (1.0 + jnp.exp(-value))


def call(kernel, out_shape, *operands, vmem, flops=0, moved=0, **more):
    return pl.pallas_call(
        kernel,
        out_shape=out_shape,
        compiler_params=pltpu.CompilerParams(vmem_limit_bytes=vmem * MIB),
        cost_estimate=pl.CostEstimate(flops=flops, bytes_accessed=moved, transcendentals=0),
        **more,
    )(*operands)


def brought(sources, held, sems):
    copies = [
        pltpu.make_async_copy(source, target, sems.at[i])
        for i, (source, target) in enumerate(zip(sources, held))
    ]
    for copy in copies:
        copy.start()
    for copy in copies:
        copy.wait()


def key_norms(key):
    key_f = key.astype(F32)
    square = key_f * key_f
    scale = lax.rsqrt(jnp.sum(square, axis=1, keepdims=True) + EPS)
    scale_row = lax.rsqrt(exact(jnp.ones((8, DK), F32), square, NT)[:1] + EPS)
    return scale, scale_row


def order(length):
    row = lax.broadcasted_iota(jnp.int32, (length, length), 0)
    col = lax.broadcasted_iota(jnp.int32, (length, length), 1)
    return row, col


def faded(on, log_col, log_row, rate_row):
    apart = jnp.where(on, log_col - log_row, 0.0)
    return jnp.where(on, jnp.exp(apart), 0.0) * rate_row


def logs(decay, on):
    tri = jnp.where(on, 1.0, 0.0)
    return -exact(decay, tri, NT), -exact(tri, decay, NT)


def solve_kernel(*refs):
    count = (len(refs) - 3) // 2
    sources, (send_ref, solved_ref) = refs[:count], refs[count : count + 2]
    held, sems = refs[count + 2 : -1], refs[-1]
    brought(sources, held, sems)
    k_ref, v_ref, decay_ref, logit_ref = held
    length = k_ref.shape[0]
    heads = decay_ref.shape[0]
    ratio = heads // (k_ref.shape[1] // DK)
    cuts = send_ref.shape[0] // heads
    rows = DV // cuts
    row, col = order(length)
    on = row >= col
    below = row > col
    eye = jnp.where(row == col, 1.0, 0.0)
    rate_row = 1.0 / (1.0 + jnp.exp(-logit_ref[...]))
    log_row, log_col = logs(decay_ref[...], on)
    rate_col = exact(eye, rate_row, NT)
    systems, keys = [], []
    for group in range(heads // ratio):
        key = k_ref[:, group * DK : (group + 1) * DK]
        scale, scale_row = key_norms(key)
        key_key = mm(key, key, NT) * (scale * scale_row)
        for head in range(group * ratio, (group + 1) * ratio):
            pick = slice(head, head + 1)
            fading = faded(on, log_col[:, pick], log_row[pick], rate_row[pick])
            systems.append(jnp.where(below, key_key * fading, 0.0))
            keys.append((key, scale))
    inverses = [eye - jnp.where(row // 2 == col // 2, system, 0.0) for system in systems]
    size = 2
    while size < length:
        lower = (row // (2 * size) == col // (2 * size)) & (row // size > col // size)
        crossing = [
            mm(jnp.where(lower, system, 0.0), inverse)
            for system, inverse in zip(systems, inverses)
        ]
        inverses = [
            inverse - mm(inverse, cross) for inverse, cross in zip(inverses, crossing)
        ]
        size *= 2
    targets = []
    for head in range(heads):
        key, scale = keys[head]
        lead = jnp.exp(log_col[:, head : head + 1])
        value = v_ref[:, head * DV : (head + 1) * DV].astype(F32)
        targets.append(jnp.concatenate([value, lead * scale * key.astype(F32)], axis=1))
    firsts = [mm(inverses[head], targets[head]) for head in range(heads)]
    missing = [
        targets[head] - firsts[head] - mm3(systems[head], firsts[head]) for head in range(heads)
    ]
    solutions = [firsts[head] + mm(inverses[head], missing[head]) for head in range(heads)]
    for head in range(heads):
        key, scale = keys[head]
        solved_ref[head] = solutions[head]
        last = log_col[length - 1 : length, head : head + 1]
        tail = jnp.exp(last - log_col[:, head : head + 1]) * rate_col[:, head : head + 1] * scale
        high, low = halves(solutions[head] * tail)
        written = mm(high, key, TN) + mm(low, key, TN)
        removed = written[DV:].astype(BF)
        added = written[:DV].astype(BF)
        fade = pieces(jnp.broadcast_to(jnp.exp(last), (MARKS, DK)))
        for cut in range(cuts):
            place = head * cuts + cut
            send_ref[place, :DK, :] = removed
            send_ref[place, DK : DK + rows, :] = added[cut * rows : (cut + 1) * rows]
            send_ref[place, DK + rows :, :] = fade


def inner_kernel(
    q_ref, k_ref, decay_ref, logit_ref, solved_ref, ids_ref, weight_ref, inside_ref, reach_ref, route_ref
):
    length = q_ref.shape[0]
    heads = decay_ref.shape[0]
    ratio = heads // (q_ref.shape[1] // DK)
    row, col = order(length)
    on = row >= col
    rate_row = 1.0 / (1.0 + jnp.exp(-logit_ref[...]))
    log_row, log_col = logs(decay_ref[...], on)
    for group in range(heads // ratio):
        part = slice(group * DK, (group + 1) * DK)
        query = q_ref[:, part]
        key = k_ref[:, part]
        query_f = query.astype(F32)
        query_scale = lax.rsqrt(jnp.sum(query_f * query_f, axis=1, keepdims=True) + EPS) * DK**-0.5
        _, scale_row = key_norms(key)
        query_key = mm(query, key, NT) * (query_scale * scale_row)
        for head in range(group * ratio, (group + 1) * ratio):
            pick = slice(head, head + 1)
            weight = query_key * faded(on, log_col[:, pick], log_row[pick], rate_row[pick])
            both = mm3(weight, solved_ref[head])
            inside_ref[head] = both[:, :DV]
            reach = jnp.exp(log_col[:, pick]) * query_scale * query_f - both[:, DV:]
            reach_ref[head] = reach.astype(BF)
    places, packed, _ = route_ref.shape
    targets = packed * 2 // 3
    number = lax.broadcasted_iota(jnp.int32, (targets, length), 0)
    number = (number // SHARES) * (places * SHARES) + number % SHARES
    for place in range(places):
        weight = jnp.zeros((targets, length), F32)
        for choice in range(ids_ref.shape[0]):
            hit = ids_ref[choice : choice + 1, :] == number + place * SHARES
            weight = weight + jnp.where(hit, weight_ref[choice : choice + 1, :], 0.0)
        weight = weight.astype(BF)
        route_ref[place, :targets, :] = weight[:, :DK]
        route_ref[place, targets:, :] = jnp.concatenate(
            [weight[: targets // 2, DK:], weight[targets // 2 :, DK:]], axis=1
        )


def total_kernel(got_ref, after_ref, total_ref):
    del after_ref
    blocks = got_ref.shape[0]
    rows = total_ref.shape[0] - DK - MARKS
    row = lax.broadcasted_iota(jnp.int32, (DK, DK), 0)
    col = lax.broadcasted_iota(jnp.int32, (DK, DK), 1)
    eye = jnp.where(row == col, 1.0, 0.0)
    whole = jnp.ones((1, DK), F32)
    product = eye
    state = jnp.zeros((rows, DK), F32)
    for block in range(blocks):
        removed, added, fade = unpack(got_ref[block], rows)
        if block == 0:
            product = fade * eye - removed.astype(F32)
            state = added
        else:
            product = advance(product, removed, fade)
            state = advance(state, removed, fade) + added
        whole = whole * fade
    total_ref[:DK, :] = (whole * eye - product).astype(BF)
    total_ref[DK : DK + rows, :] = state.astype(BF)
    total_ref[DK + rows :, :] = pieces(jnp.broadcast_to(whole, (MARKS, DK)))


def state_kernel(here_ref, got_ref, route_ref, *rest):
    totals, enter_ref = rest[:-1], rest[-1]
    blocks = enter_ref.shape[0]
    rows = enter_ref.shape[1] - route_ref.shape[1]
    enter_ref[:, rows:, :] = route_ref[...]
    state = jnp.zeros((rows, DK), F32)
    for distance in range(len(totals), 0, -1):
        removed, added, fade = unpack(totals[distance - 1], rows)
        state = jnp.where(distance <= here_ref[0], advance(state, removed, fade) + added, state)
    for block in range(blocks):
        enter_ref[block, :rows, :] = state.astype(BF)
        if block < blocks - 1:
            removed, added, fade = unpack(got_ref[block], rows)
            state = advance(state, removed, fade) + added


def output_kernel(
    here_ref, inside_ref, reach_ref, state_ref, gate_ref, gain_ref, proj_ref, rest_ref, keep_ref, give_ref
):
    heads = inside_ref.shape[0]
    gated = []
    for head in range(heads):
        part = slice(head * DV, (head + 1) * DV)
        cuts = state_ref.shape[0] // heads
        places = range(head * cuts, (head + 1) * cuts)
        state = jnp.concatenate([state_ref[place, : DV // cuts] for place in places], axis=0)
        output = inside_ref[head] + mm(reach_ref[head], state, NT)
        scaling = lax.rsqrt(jnp.mean(output * output, axis=1, keepdims=True) + EPS)
        opened = silu(gate_ref[:, part].astype(F32))
        gated.append((output * scaling * gain_ref[...] * opened).astype(BF))
    gated = jnp.concatenate(gated, axis=1)
    columns, _, width = keep_ref.shape
    for distance in range(columns):
        column = lax.rem(here_ref[2] + distance, columns)
        for core, out_ref in ((here_ref[3], keep_ref), (1 - here_ref[3], give_ref)):
            first = pl.multiple_of((column * 2 + core) * width, width)
            mixed = mm(gated, proj_ref[:, pl.ds(first, width)])
            if distance == 0 and out_ref is keep_ref:
                mixed = mixed + rest_ref[:, pl.ds(first, width)].astype(F32)
            out_ref[distance] = mixed.astype(out_ref.dtype)


def route_kernel(here_ref, got_ref, pick_ref, mix_ref):
    blocks, slots, length = pick_ref.shape
    targets = slots // SLOTS
    base = got_ref.shape[1] - targets - targets // 2
    iota = lambda shape, dim: lax.broadcasted_iota(jnp.int32, shape, dim)
    earlier = (iota((length, length), 0) > iota((length, length), 1)).astype(BF)
    earlier_t = (iota((length, length), 0) < iota((length, length), 1)).astype(BF)
    eye = (iota((length, length), 0) == iota((length, length), 1)).astype(BF)
    spread = (iota((targets, slots), 1) // SLOTS == iota((targets, slots), 0)).astype(BF)
    spread_t = (iota((slots, targets), 0) // SLOTS == iota((slots, targets), 1)).astype(BF)
    slot = (iota((length, slots), 1) % SLOTS).astype(F32)
    slot_t = (iota((slots, length), 0) % SLOTS).astype(F32)
    for block in range(blocks):
        source = lax.rem(here_ref[1] + blocks - block, blocks)
        first = got_ref[source, base : base + targets, :]
        last = got_ref[source, base + targets :, :]
        rest = length - DK
        last = jnp.concatenate([last[:, :rest], last[:, rest:]], axis=0)
        weight_t = jnp.concatenate([first, last], axis=1)
        named_t = weight_t.astype(F32) > 0.0
        weight = mm(eye, weight_t, NT)
        named = weight > 0.0
        place = jnp.where(named, mm(earlier, jnp.where(named, 1.0, 0.0)), -1.0)
        place_t = jnp.where(named_t, mm(jnp.where(named_t, 1.0, 0.0), earlier_t), -1.0)
        mix_ref[block] = jnp.where(mm(place, spread) == slot, mm(weight, spread), 0.0).astype(BF)
        pick_ref[block] = jnp.where(mm(spread_t, place_t) == slot_t, 1.0, 0.0).astype(BF)


def pick_kernel(pick_ref, *rest):
    tokens, send_ref = rest[:-1], rest[-1]
    targets = send_ref.shape[0]
    width = send_ref.shape[2]
    for block in range(pick_ref.shape[0]):
        rows = mm(pick_ref[block], tokens[block][...]).astype(BF)
        send_ref[:, block * SLOTS : (block + 1) * SLOTS, :] = rows.reshape(targets, SLOTS, width)


def expert_kernel(rows_ref, gain_ref, gate_ref, up_ref, down_ref, out_ref, normed_ref):
    groups, shares, count, width = rows_ref.shape
    for group in range(groups):
        place = slice(group * count, (group + 1) * count)
        total = jnp.zeros((count, 1), F32)
        for share in range(shares):
            piece = rows_ref[group, share].astype(F32)
            total = total + jnp.sum(piece * piece, axis=1, keepdims=True)
        scaling = lax.rsqrt(total / (shares * width) + EPS)
        for share in range(shares):
            part = slice(share * width, (share + 1) * width)
            piece = rows_ref[group, share].astype(F32)
            normed_ref[place, part] = (piece * scaling * gain_ref[:, part]).astype(BF)
    normed = normed_ref[...]
    hidden = (silu(mm(normed, gate_ref[...])) * mm(normed, up_ref[...])).astype(BF)
    for share in range(shares):
        part = slice(share * width, (share + 1) * width)
        produced = mm(hidden, down_ref[:, part]).astype(BF)
        for group in range(groups):
            out_ref[group, share] = produced[group * count : (group + 1) * count]


def combine_kernel(mix_ref, rows_ref, *outs):
    targets, _, width = rows_ref.shape
    for block in range(mix_ref.shape[0]):
        rows = rows_ref[:, block * SLOTS : (block + 1) * SLOTS, :].reshape(targets * SLOTS, width)
        outs[block][...] = mm(mix_ref[block], rows).astype(outs[block].dtype)


SCALAR = pl.BlockSpec(memory_space=pltpu.SMEM)
VECTOR = pl.BlockSpec(memory_space=pltpu.VMEM)
UNREAD = pl.BlockSpec(memory_space=pl.ANY)
REMOTE = pl.BlockSpec(memory_space=pltpu.HBM)


def shifted(value, axis, distance):
    size = lax.axis_size(axis)
    return lax.ppermute(value, axis, [(i, (i + distance) % size) for i in range(size)])


def swap(value, axes):
    return lax.all_to_all(value, axes, 0, 0, tiled=True)


def spread_out(value, axis):
    right = [value, shifted(value, axis, 1), shifted(value, axis, 2)]
    left = [shifted(value, axis, -1), shifted(value, axis, -2)]
    right.append(shifted(right[2], axis, 1))
    left.append(shifted(left[1], axis, -1))
    left.append(shifted(left[1], axis, -2))
    return right + left[::-1]


def gathered_sum(parts, axis):
    def passed(value, distance):
        return shifted(value.astype(BF), axis, distance).astype(F32)

    left = parts[2] + passed(parts[3], -1) + passed(parts[4], -2)
    right = parts[6] + passed(parts[5], 1)
    right, first, last = lax.optimization_barrier((right, parts[1], parts[7]))
    near = passed(first, -1) + passed(last, 1)
    return parts[0] + near + (passed(left, -2) + passed(right, 2))


def on_device(
    query_in,
    key_in,
    value_in,
    gate_in,
    decay_rate,
    beta_logit,
    head_gain,
    out_proj,
    residual_in,
    post_gain,
    expert_ids,
    route_weight,
    w_gate,
    w_up,
    w_down,
):
    length = query_in.shape[0]
    heads = decay_rate.shape[0]
    blocks = lax.axis_size("z")
    groups = lax.axis_size("x")
    shares = lax.axis_size("y") * lax.axis_size("c")
    width = residual_in.shape[1] // shares
    count = blocks * SLOTS
    targets = groups * shares
    shape = jax.ShapeDtypeStruct

    rows = heads * DV // blocks
    extra = targets + targets // 2
    here = jnp.stack([lax.axis_index(axis) for axis in ("x", "z", "y", "c")])
    operands = (key_in, value_in, decay_rate, beta_logit)
    send, solved = call(
        solve_kernel,
        (
            shape((blocks, DK + rows + MARKS, DK), BF),
            shape((heads, length, DV + DK), F32),
        ),
        *operands,
        vmem=62,
        in_specs=[REMOTE] * len(operands),
        scratch_shapes=[pltpu.VMEM(item.shape, item.dtype) for item in operands]
        + [pltpu.SemaphoreType.DMA((len(operands),))],
    )
    got = swap(send, "z")
    inside, reach, route = call(
        inner_kernel,
        (
            shape((heads, length, DV), F32),
            shape((heads, length, DK), BF),
            shape((blocks, extra, DK), BF),
        ),
        query_in,
        key_in,
        decay_rate,
        beta_logit,
        solved,
        expert_ids.T,
        route_weight.T,
        vmem=16,
        flops=2 * 10**9,
        moved=3 * 10**6,
    )
    total = call(
        total_kernel,
        shape((DK + rows + MARKS, DK), BF),
        got,
        route,
        vmem=8,
        in_specs=[VECTOR, UNREAD],
    )
    totals = [shifted(total, "x", distance) for distance in range(1, groups)]
    enter = call(
        state_kernel,
        shape((blocks, rows + extra, DK), BF),
        here,
        got,
        route,
        *totals,
        vmem=8,
        in_specs=[SCALAR] + [VECTOR] * (2 + len(totals)),
    )
    back = swap(enter, "z")
    pick, mix = call(
        route_kernel,
        (
            shape((blocks, targets * SLOTS, length), BF),
            shape((blocks, length, targets * SLOTS), BF),
        ),
        here,
        back,
        vmem=12,
        flops=10**9,
        moved=4 * 10**6,
        in_specs=[SCALAR, VECTOR],
    )

    columns = lax.axis_size("y")
    keep, give = call(
        output_kernel,
        (shape((columns, length, width), F32), shape((columns, length, width), BF)),
        here,
        inside,
        reach,
        back,
        gate_in,
        head_gain.reshape(1, DV),
        out_proj,
        residual_in,
        vmem=16,
        in_specs=[SCALAR] + [VECTOR] * 7,
    )
    both = keep + shifted(give, "c", 1).astype(F32)
    mixed = both[0]
    for distance in range(1, columns):
        mixed = mixed + shifted(both[distance].astype(BF), "y", distance).astype(F32)
    middle = mixed.astype(BF)

    tokens = spread_out(middle, "z")
    send = call(pick_kernel, shape((targets, count, width), BF), pick, *tokens, vmem=12)
    arrived = swap(send, ("x", "y", "c")).reshape(groups, shares, count, width)
    produced = call(
        expert_kernel,
        shape((groups, shares, count, width), BF),
        arrived,
        post_gain.reshape(1, -1),
        w_gate[0],
        w_up[0],
        w_down[0],
        vmem=24,
        scratch_shapes=[pltpu.VMEM((groups * count, shares * width), BF)],
    )
    returned = swap(produced.reshape(targets, count, width), ("x", "y", "c"))
    mixes = call(
        combine_kernel,
        tuple(shape((length, width), F32 if i in (0, 2, 6) else BF) for i in range(blocks)),
        mix,
        returned,
        vmem=16,
    )
    expert_mix = gathered_sum(mixes, "z")
    layer_out = (middle.astype(F32) + expert_mix).astype(BF)
    return (middle, layer_out)


def solution(mesh):
    ctx, exp = mesh.devices.shape
    split = Mesh(mesh.devices.reshape(4, ctx // 4, exp // 2, 2), ("x", "z", "y", "c"))
    row, col = ("x", "z"), ("y", "c")
    in_specs = (
        P(row, col),
        P(row, col),
        P(row, col),
        P(row, col),
        P(col, row),
        P(col, row),
        P(),
        P(col, None),
        P(row, None),
        P(),
        P(row, None),
        P(row, None),
        P(row + col, None, None),
        P(row + col, None, None),
        P(row + col, None, None),
    )
    out_specs = (P(row, col), P(row, col))
    return jax.shard_map(
        on_device, mesh=split, in_specs=in_specs, out_specs=out_specs, check_vma=False
    )
```

```python
import functools

import jax
import jax.numpy as jnp
from jax import lax
from jax.experimental import pallas as pl
from jax.experimental.pallas import tpu as pltpu
from jax.sharding import Mesh, PartitionSpec as P

DK = 128
DV = 128
SLOTS = 16
MARKS = 16
SHARES = 8
EPS = 1e-06
BF = jnp.bfloat16
F32 = jnp.float32
NN = ((1,), (0,))
NT = ((1,), (1,))
TN = ((0,), (0,))
MIB = 1024 * 1024


def mm(left, right, dims=NN):
    return lax.dot_general(
        left.astype(BF), right.astype(BF), (dims, ((), ())), preferred_element_type=F32
    )


def exact(left, right, dims=NN):
    return lax.dot_general(
        left, right, (dims, ((), ())), precision=lax.Precision.HIGHEST, preferred_element_type=F32
    )


def halves(value):
    high = value.astype(BF)
    return high, (value - high.astype(F32)).astype(BF)


def mm3(left, right, dims=NN):
    left_high, left_low = halves(left)
    right_high, right_low = halves(right)
    return (
        mm(left_high, right_high, dims)
        + mm(left_high, right_low, dims)
        + mm(left_low, right_high, dims)
    )


def pieces(value):
    first, second = halves(value)
    third = (value - first.astype(F32) - second.astype(F32)).astype(BF)
    row = lax.broadcasted_iota(jnp.int32, value.shape, 0)
    return jnp.where(row == 0, first, jnp.where(row == 1, second, third))


def joined(marks):
    marks = marks.astype(F32)
    return marks[0:1] + marks[1:2] + marks[2:3]


def unpack(got, rows):
    fade = joined(got[DK + rows : DK + rows + MARKS, :])
    return got[:DK, :], got[DK : DK + rows, :].astype(F32), fade


def advance(state, removed, fade):
    high, low = halves(state)
    return fade * state - (mm(high, removed) + mm(low, removed))


def silu(value):
    return value / (1.0 + jnp.exp(-value))


def call(kernel, out_shape, *operands, vmem, flops=0, moved=0, **more):
    return pl.pallas_call(
        kernel,
        out_shape=out_shape,
        compiler_params=pltpu.CompilerParams(vmem_limit_bytes=vmem * MIB),
        cost_estimate=pl.CostEstimate(flops=flops, bytes_accessed=moved, transcendentals=0),
        **more,
    )(*operands)


def brought(sources, held, sems):
    copies = [
        pltpu.make_async_copy(source, target, sems.at[i])
        for i, (source, target) in enumerate(zip(sources, held))
    ]
    for copy in copies:
        copy.start()
    for copy in copies:
        copy.wait()


def key_norms(key):
    key_f = key.astype(F32)
    square = key_f * key_f
    scale = lax.rsqrt(jnp.sum(square, axis=1, keepdims=True) + EPS)
    scale_row = lax.rsqrt(exact(jnp.ones((8, DK), F32), square, NT)[:1] + EPS)
    return scale, scale_row


def order(length):
    row = lax.broadcasted_iota(jnp.int32, (length, length), 0)
    col = lax.broadcasted_iota(jnp.int32, (length, length), 1)
    return row, col


def faded(on, log_col, log_row, rate_row):
    apart = jnp.where(on, log_col - log_row, 0.0)
    return jnp.where(on, jnp.exp(apart), 0.0) * rate_row


def logs(decay, on):
    tri = jnp.where(on, 1.0, 0.0)
    return -exact(decay, tri, NT), -exact(tri, decay, NT)


def solve_kernel(*refs):
    count = (len(refs) - 3) // 2
    sources, (send_ref, solved_ref) = refs[:count], refs[count : count + 2]
    held, sems = refs[count + 2 : -1], refs[-1]
    brought(sources, held, sems)
    k_ref, v_ref, decay_ref, logit_ref = held
    length = k_ref.shape[0]
    heads = decay_ref.shape[0]
    ratio = heads // (k_ref.shape[1] // DK)
    cuts = send_ref.shape[0] // heads
    rows = DV // cuts
    row, col = order(length)
    on = row >= col
    below = row > col
    eye = jnp.where(row == col, 1.0, 0.0)
    rate_row = 1.0 / (1.0 + jnp.exp(-logit_ref[...]))
    log_row, log_col = logs(decay_ref[...], on)
    rate_col = exact(eye, rate_row, NT)
    systems, keys = [], []
    for group in range(heads // ratio):
        key = k_ref[:, group * DK : (group + 1) * DK]
        scale, scale_row = key_norms(key)
        key_key = mm(key, key, NT) * (scale * scale_row)
        for head in range(group * ratio, (group + 1) * ratio):
            pick = slice(head, head + 1)
            fading = faded(on, log_col[:, pick], log_row[pick], rate_row[pick])
            systems.append(jnp.where(below, key_key * fading, 0.0))
            keys.append((key, scale))
    inverses = [eye - jnp.where(row // 2 == col // 2, system, 0.0) for system in systems]
    size = 2
    while size < length:
        lower = (row // (2 * size) == col // (2 * size)) & (row // size > col // size)
        crossing = [
            mm(jnp.where(lower, system, 0.0), inverse)
            for system, inverse in zip(systems, inverses)
        ]
        inverses = [
            inverse - mm(inverse, cross) for inverse, cross in zip(inverses, crossing)
        ]
        size *= 2
    targets = []
    for head in range(heads):
        key, scale = keys[head]
        lead = jnp.exp(log_col[:, head : head + 1])
        value = v_ref[:, head * DV : (head + 1) * DV].astype(F32)
        targets.append(jnp.concatenate([value, lead * scale * key.astype(F32)], axis=1))
    firsts = [mm(inverses[head], targets[head]) for head in range(heads)]
    missing = [
        targets[head] - firsts[head] - mm3(systems[head], firsts[head]) for head in range(heads)
    ]
    solutions = [firsts[head] + mm(inverses[head], missing[head]) for head in range(heads)]
    for head in range(heads):
        key, scale = keys[head]
        solved_ref[head] = solutions[head]
        last = log_col[length - 1 : length, head : head + 1]
        tail = jnp.exp(last - log_col[:, head : head + 1]) * rate_col[:, head : head + 1] * scale
        high, low = halves(solutions[head] * tail)
        written = mm(high, key, TN) + mm(low, key, TN)
        removed = written[DV:].astype(BF)
        added = written[:DV].astype(BF)
        fade = pieces(jnp.broadcast_to(jnp.exp(last), (MARKS, DK)))
        for cut in range(cuts):
            place = head * cuts + cut
            send_ref[place, :DK, :] = removed
            send_ref[place, DK : DK + rows, :] = added[cut * rows : (cut + 1) * rows]
            send_ref[place, DK + rows :, :] = fade


def inner_kernel(
    q_ref, k_ref, decay_ref, logit_ref, solved_ref, ids_ref, weight_ref, inside_ref, reach_ref, route_ref
):
    length = q_ref.shape[0]
    heads = decay_ref.shape[0]
    ratio = heads // (q_ref.shape[1] // DK)
    row, col = order(length)
    on = row >= col
    rate_row = 1.0 / (1.0 + jnp.exp(-logit_ref[...]))
    log_row, log_col = logs(decay_ref[...], on)
    for group in range(heads // ratio):
        part = slice(group * DK, (group + 1) * DK)
        query = q_ref[:, part]
        key = k_ref[:, part]
        query_f = query.astype(F32)
        query_scale = lax.rsqrt(jnp.sum(query_f * query_f, axis=1, keepdims=True) + EPS) * DK**-0.5
        _, scale_row = key_norms(key)
        query_key = mm(query, key, NT) * (query_scale * scale_row)
        for head in range(group * ratio, (group + 1) * ratio):
            pick = slice(head, head + 1)
            weight = query_key * faded(on, log_col[:, pick], log_row[pick], rate_row[pick])
            both = mm3(weight, solved_ref[head])
            inside_ref[head] = both[:, :DV]
            reach = jnp.exp(log_col[:, pick]) * query_scale * query_f - both[:, DV:]
            reach_ref[head] = reach.astype(BF)
    places, packed, _ = route_ref.shape
    targets = packed * 2 // 3
    number = lax.broadcasted_iota(jnp.int32, (targets, length), 0)
    number = (number // SHARES) * (places * SHARES) + number % SHARES
    for place in range(places):
        weight = jnp.zeros((targets, length), F32)
        for choice in range(ids_ref.shape[0]):
            hit = ids_ref[choice : choice + 1, :] == number + place * SHARES
            weight = weight + jnp.where(hit, weight_ref[choice : choice + 1, :], 0.0)
        weight = weight.astype(BF)
        route_ref[place, :targets, :] = weight[:, :DK]
        route_ref[place, targets:, :] = jnp.concatenate(
            [weight[: targets // 2, DK:], weight[targets // 2 :, DK:]], axis=1
        )


def total_kernel(got_ref, after_ref, total_ref):
    del after_ref
    blocks = got_ref.shape[0]
    rows = total_ref.shape[0] - DK - MARKS
    row = lax.broadcasted_iota(jnp.int32, (DK, DK), 0)
    col = lax.broadcasted_iota(jnp.int32, (DK, DK), 1)
    eye = jnp.where(row == col, 1.0, 0.0)
    whole = jnp.ones((1, DK), F32)
    product = eye
    state = jnp.zeros((rows, DK), F32)
    for block in range(blocks):
        removed, added, fade = unpack(got_ref[block], rows)
        if block == 0:
            product = fade * eye - removed.astype(F32)
            state = added
        else:
            product = advance(product, removed, fade)
            state = advance(state, removed, fade) + added
        whole = whole * fade
    total_ref[:DK, :] = (whole * eye - product).astype(BF)
    total_ref[DK : DK + rows, :] = state.astype(BF)
    total_ref[DK + rows :, :] = pieces(jnp.broadcast_to(whole, (MARKS, DK)))


def state_kernel(here_ref, got_ref, route_ref, *rest):
    totals, enter_ref = rest[:-1], rest[-1]
    blocks = enter_ref.shape[0]
    rows = enter_ref.shape[1] - route_ref.shape[1]
    enter_ref[:, rows:, :] = route_ref[...]
    state = jnp.zeros((rows, DK), F32)
    for distance in range(len(totals), 0, -1):
        removed, added, fade = unpack(totals[distance - 1], rows)
        state = jnp.where(distance <= here_ref[0], advance(state, removed, fade) + added, state)
    for block in range(blocks):
        enter_ref[block, :rows, :] = state.astype(BF)
        if block < blocks - 1:
            removed, added, fade = unpack(got_ref[block], rows)
            state = advance(state, removed, fade) + added


def output_kernel(
    here_ref, inside_ref, reach_ref, state_ref, gate_ref, gain_ref, proj_ref, rest_ref, keep_ref, give_ref
):
    heads = inside_ref.shape[0]
    gated = []
    for head in range(heads):
        part = slice(head * DV, (head + 1) * DV)
        cuts = state_ref.shape[0] // heads
        places = range(head * cuts, (head + 1) * cuts)
        state = jnp.concatenate([state_ref[place, : DV // cuts] for place in places], axis=0)
        output = inside_ref[head] + mm(reach_ref[head], state, NT)
        scaling = lax.rsqrt(jnp.mean(output * output, axis=1, keepdims=True) + EPS)
        opened = silu(gate_ref[:, part].astype(F32))
        gated.append((output * scaling * gain_ref[...] * opened).astype(BF))
    gated = jnp.concatenate(gated, axis=1)
    columns, _, width = keep_ref.shape
    for distance in range(columns):
        column = lax.rem(here_ref[2] + distance, columns)
        for core, out_ref in ((here_ref[3], keep_ref), (1 - here_ref[3], give_ref)):
            first = pl.multiple_of((column * 2 + core) * width, width)
            mixed = mm(gated, proj_ref[:, pl.ds(first, width)])
            if distance == 0 and out_ref is keep_ref:
                mixed = mixed + rest_ref[:, pl.ds(first, width)].astype(F32)
            out_ref[distance] = mixed.astype(out_ref.dtype)


def route_kernel(here_ref, got_ref, pick_ref, mix_ref):
    blocks, slots, length = pick_ref.shape
    targets = slots // SLOTS
    base = got_ref.shape[1] - targets - targets // 2
    iota = lambda shape, dim: lax.broadcasted_iota(jnp.int32, shape, dim)
    earlier = (iota((length, length), 0) > iota((length, length), 1)).astype(BF)
    earlier_t = (iota((length, length), 0) < iota((length, length), 1)).astype(BF)
    eye = (iota((length, length), 0) == iota((length, length), 1)).astype(BF)
    spread = (iota((targets, slots), 1) // SLOTS == iota((targets, slots), 0)).astype(BF)
    spread_t = (iota((slots, targets), 0) // SLOTS == iota((slots, targets), 1)).astype(BF)
    slot = (iota((length, slots), 1) % SLOTS).astype(F32)
    slot_t = (iota((slots, length), 0) % SLOTS).astype(F32)
    for block in range(blocks):
        source = lax.rem(here_ref[1] + blocks - block, blocks)
        first = got_ref[source, base : base + targets, :]
        last = got_ref[source, base + targets :, :]
        rest = length - DK
        last = jnp.concatenate([last[:, :rest], last[:, rest:]], axis=0)
        weight_t = jnp.concatenate([first, last], axis=1)
        named_t = weight_t.astype(F32) > 0.0
        weight = mm(eye, weight_t, NT)
        named = weight > 0.0
        place = jnp.where(named, mm(earlier, jnp.where(named, 1.0, 0.0)), -1.0)
        place_t = jnp.where(named_t, mm(jnp.where(named_t, 1.0, 0.0), earlier_t), -1.0)
        mix_ref[block] = jnp.where(mm(place, spread) == slot, mm(weight, spread), 0.0).astype(BF)
        pick_ref[block] = jnp.where(mm(spread_t, place_t) == slot_t, 1.0, 0.0).astype(BF)


def pick_kernel(pick_ref, *rest):
    tokens, send_ref = rest[:-1], rest[-1]
    targets = send_ref.shape[0]
    width = send_ref.shape[2]
    for block in range(pick_ref.shape[0]):
        rows = mm(pick_ref[block], tokens[block][...]).astype(BF)
        send_ref[:, block * SLOTS : (block + 1) * SLOTS, :] = rows.reshape(targets, SLOTS, width)


def expert_kernel(rows_ref, gain_ref, gate_ref, up_ref, down_ref, out_ref, normed_ref):
    groups, shares, count, width = rows_ref.shape
    for group in range(groups):
        place = slice(group * count, (group + 1) * count)
        total = jnp.zeros((count, 1), F32)
        for share in range(shares):
            piece = rows_ref[group, share].astype(F32)
            total = total + jnp.sum(piece * piece, axis=1, keepdims=True)
        scaling = lax.rsqrt(total / (shares * width) + EPS)
        for share in range(shares):
            part = slice(share * width, (share + 1) * width)
            piece = rows_ref[group, share].astype(F32)
            normed_ref[place, part] = (piece * scaling * gain_ref[:, part]).astype(BF)
    normed = normed_ref[...]
    hidden = (silu(mm(normed, gate_ref[...])) * mm(normed, up_ref[...])).astype(BF)
    for share in range(shares):
        part = slice(share * width, (share + 1) * width)
        produced = mm(hidden, down_ref[:, part]).astype(BF)
        for group in range(groups):
            out_ref[group, share] = produced[group * count : (group + 1) * count]


def combine_kernel(mix_ref, rows_ref, *outs):
    targets, _, width = rows_ref.shape
    for block in range(mix_ref.shape[0]):
        rows = rows_ref[:, block * SLOTS : (block + 1) * SLOTS, :].reshape(targets * SLOTS, width)
        outs[block][...] = mm(mix_ref[block], rows).astype(outs[block].dtype)


SCALAR = pl.BlockSpec(memory_space=pltpu.SMEM)
VECTOR = pl.BlockSpec(memory_space=pltpu.VMEM)
UNREAD = pl.BlockSpec(memory_space=pl.ANY)
REMOTE = pl.BlockSpec(memory_space=pltpu.HBM)


def shifted(value, axis, distance):
    size = lax.axis_size(axis)
    return lax.ppermute(value, axis, [(i, (i + distance) % size) for i in range(size)])


def swap(value, axes):
    return lax.all_to_all(value, axes, 0, 0, tiled=True)


def spread_out(value, axis):
    right = [value, shifted(value, axis, 1), shifted(value, axis, 2)]
    left = [shifted(value, axis, -1), shifted(value, axis, -2)]
    far = shifted(left[1], axis, -2)
    left.append(shifted(left[1], axis, -1))
    right.append(shifted(right[2], axis, 1))
    left.append(far)
    return right + left[::-1]


def gathered_sum(parts, axis):
    def passed(value, distance):
        return shifted(value.astype(BF), axis, distance).astype(F32)

    left = parts[2] + passed(parts[4], -2) + passed(parts[3], -1)
    right = parts[6] + passed(parts[5], 1)
    right, first, last = lax.optimization_barrier((right, parts[1], parts[7]))
    near = passed(first, -1) + passed(last, 1)
    return parts[0] + near + (passed(left, -2) + passed(right, 2))


def on_device(
    query_in,
    key_in,
    value_in,
    gate_in,
    decay_rate,
    beta_logit,
    head_gain,
    out_proj,
    residual_in,
    post_gain,
    expert_ids,
    route_weight,
    w_gate,
    w_up,
    w_down,
):
    length = query_in.shape[0]
    heads = decay_rate.shape[0]
    blocks = lax.axis_size("z")
    groups = lax.axis_size("x")
    shares = lax.axis_size("y") * lax.axis_size("c")
    width = residual_in.shape[1] // shares
    count = blocks * SLOTS
    targets = groups * shares
    shape = jax.ShapeDtypeStruct

    rows = heads * DV // blocks
    extra = targets + targets // 2
    here = jnp.stack([lax.axis_index(axis) for axis in ("x", "z", "y", "c")])
    operands = (key_in, value_in, decay_rate, beta_logit)
    send, solved = call(
        solve_kernel,
        (
            shape((blocks, DK + rows + MARKS, DK), BF),
            shape((heads, length, DV + DK), F32),
        ),
        *operands,
        vmem=62,
        in_specs=[REMOTE] * len(operands),
        scratch_shapes=[pltpu.VMEM(item.shape, item.dtype) for item in operands]
        + [pltpu.SemaphoreType.DMA((len(operands),))],
    )
    got = swap(send, "z")
    inside, reach, route = call(
        inner_kernel,
        (
            shape((heads, length, DV), F32),
            shape((heads, length, DK), BF),
            shape((blocks, extra, DK), BF),
        ),
        query_in,
        key_in,
        decay_rate,
        beta_logit,
        solved,
        expert_ids.T,
        route_weight.T,
        vmem=16,
        flops=2 * 10**9,
        moved=3 * 10**6,
    )
    total = call(
        total_kernel,
        shape((DK + rows + MARKS, DK), BF),
        got,
        route,
        vmem=8,
        in_specs=[VECTOR, UNREAD],
    )
    totals = [shifted(total, "x", distance) for distance in range(1, groups)]
    enter = call(
        state_kernel,
        shape((blocks, rows + extra, DK), BF),
        here,
        got,
        route,
        *totals,
        vmem=8,
        in_specs=[SCALAR] + [VECTOR] * (2 + len(totals)),
    )
    back = swap(enter, "z")
    pick, mix = call(
        route_kernel,
        (
            shape((blocks, targets * SLOTS, length), BF),
            shape((blocks, length, targets * SLOTS), BF),
        ),
        here,
        back,
        vmem=12,
        flops=10**9,
        moved=4 * 10**6,
        in_specs=[SCALAR, VECTOR],
    )

    columns = lax.axis_size("y")
    keep, give = call(
        output_kernel,
        (shape((columns, length, width), F32), shape((columns, length, width), BF)),
        here,
        inside,
        reach,
        back,
        gate_in,
        head_gain.reshape(1, DV),
        out_proj,
        residual_in,
        vmem=16,
        in_specs=[SCALAR] + [VECTOR] * 7,
    )
    both = keep + shifted(give, "c", 1).astype(F32)
    mixed = both[0]
    for distance in range(1, columns):
        mixed = mixed + shifted(both[distance].astype(BF), "y", distance).astype(F32)
    middle = mixed.astype(BF)

    tokens = spread_out(middle, "z")
    send = call(pick_kernel, shape((targets, count, width), BF), pick, *tokens, vmem=12)
    arrived = swap(send, ("x", "y", "c")).reshape(groups, shares, count, width)
    produced = call(
        expert_kernel,
        shape((groups, shares, count, width), BF),
        arrived,
        post_gain.reshape(1, -1),
        w_gate[0],
        w_up[0],
        w_down[0],
        vmem=24,
        scratch_shapes=[pltpu.VMEM((groups * count, shares * width), BF)],
    )
    returned = swap(produced.reshape(targets, count, width), ("x", "y", "c"))
    mixes = call(
        combine_kernel,
        tuple(shape((length, width), F32 if i in (0, 2, 6) else BF) for i in range(blocks)),
        mix,
        returned,
        vmem=16,
    )
    expert_mix = gathered_sum(mixes, "z")
    layer_out = (middle.astype(F32) + expert_mix).astype(BF)
    return (middle, layer_out)


def solution(mesh):
    ctx, exp = mesh.devices.shape
    split = Mesh(mesh.devices.reshape(4, ctx // 4, exp // 2, 2), ("x", "z", "y", "c"))
    row, col = ("x", "z"), ("y", "c")
    in_specs = (
        P(row, col),
        P(row, col),
        P(row, col),
        P(row, col),
        P(col, row),
        P(col, row),
        P(),
        P(col, None),
        P(row, None),
        P(),
        P(row, None),
        P(row, None),
        P(row + col, None, None),
        P(row + col, None, None),
        P(row + col, None, None),
    )
    out_specs = (P(row, col), P(row, col))
    return jax.shard_map(
        on_device, mesh=split, in_specs=in_specs, out_specs=out_specs, check_vma=False
    )
```

```python
import functools

import jax
import jax.numpy as jnp
from jax import lax
from jax.experimental import pallas as pl
from jax.experimental.pallas import tpu as pltpu
from jax.sharding import Mesh, PartitionSpec as P

DK = 128
DV = 128
SLOTS = 16
MARKS = 16
SHARES = 8
EPS = 1e-06
BF = jnp.bfloat16
F32 = jnp.float32
NN = ((1,), (0,))
NT = ((1,), (1,))
TN = ((0,), (0,))
MIB = 1024 * 1024


def mm(left, right, dims=NN):
    return lax.dot_general(
        left.astype(BF), right.astype(BF), (dims, ((), ())), preferred_element_type=F32
    )


def exact(left, right, dims=NN):
    return lax.dot_general(
        left, right, (dims, ((), ())), precision=lax.Precision.HIGHEST, preferred_element_type=F32
    )


def halves(value):
    high = value.astype(BF)
    return high, (value - high.astype(F32)).astype(BF)


def mm3(left, right, dims=NN):
    left_high, left_low = halves(left)
    right_high, right_low = halves(right)
    return (
        mm(left_high, right_high, dims)
        + mm(left_high, right_low, dims)
        + mm(left_low, right_high, dims)
    )


def pieces(value):
    first, second = halves(value)
    third = (value - first.astype(F32) - second.astype(F32)).astype(BF)
    row = lax.broadcasted_iota(jnp.int32, value.shape, 0)
    return jnp.where(row == 0, first, jnp.where(row == 1, second, third))


def joined(marks):
    marks = marks.astype(F32)
    return marks[0:1] + marks[1:2] + marks[2:3]


def unpack(got, rows):
    fade = joined(got[DK + rows : DK + rows + MARKS, :])
    return got[:DK, :], got[DK : DK + rows, :].astype(F32), fade


def advance(state, removed, fade):
    high, low = halves(state)
    return fade * state - (mm(high, removed) + mm(low, removed))


def silu(value):
    return value / (1.0 + jnp.exp(-value))


def call(kernel, out_shape, *operands, vmem, flops=0, moved=0, **more):
    return pl.pallas_call(
        kernel,
        out_shape=out_shape,
        compiler_params=pltpu.CompilerParams(vmem_limit_bytes=vmem * MIB),
        cost_estimate=pl.CostEstimate(flops=flops, bytes_accessed=moved, transcendentals=0),
        **more,
    )(*operands)


def brought(sources, held, sems):
    copies = [
        pltpu.make_async_copy(source, target, sems.at[i])
        for i, (source, target) in enumerate(zip(sources, held))
    ]
    for copy in copies:
        copy.start()
    for copy in copies:
        copy.wait()


def key_norms(key):
    key_f = key.astype(F32)
    square = key_f * key_f
    scale = lax.rsqrt(jnp.sum(square, axis=1, keepdims=True) + EPS)
    scale_row = lax.rsqrt(exact(jnp.ones((8, DK), F32), square, NT)[:1] + EPS)
    return scale, scale_row


def order(length):
    row = lax.broadcasted_iota(jnp.int32, (length, length), 0)
    col = lax.broadcasted_iota(jnp.int32, (length, length), 1)
    return row, col


def faded(on, log_col, log_row, rate_row):
    apart = jnp.where(on, log_col - log_row, 0.0)
    return jnp.where(on, jnp.exp(apart), 0.0) * rate_row


def logs(decay, on):
    tri = jnp.where(on, 1.0, 0.0)
    return -exact(decay, tri, NT), -exact(tri, decay, NT)


def solve_kernel(*refs):
    count = (len(refs) - 3) // 2
    sources, (send_ref, solved_ref) = refs[:count], refs[count : count + 2]
    held, sems = refs[count + 2 : -1], refs[-1]
    brought(sources, held, sems)
    k_ref, v_ref, decay_ref, logit_ref = held
    length = k_ref.shape[0]
    heads = decay_ref.shape[0]
    ratio = heads // (k_ref.shape[1] // DK)
    cuts = send_ref.shape[0] // heads
    rows = DV // cuts
    row, col = order(length)
    on = row >= col
    below = row > col
    eye = jnp.where(row == col, 1.0, 0.0)
    rate_row = 1.0 / (1.0 + jnp.exp(-logit_ref[...]))
    log_row, log_col = logs(decay_ref[...], on)
    rate_col = exact(eye, rate_row, NT)
    systems, keys = [], []
    for group in range(heads // ratio):
        key = k_ref[:, group * DK : (group + 1) * DK]
        scale, scale_row = key_norms(key)
        key_key = mm(key, key, NT) * (scale * scale_row)
        for head in range(group * ratio, (group + 1) * ratio):
            pick = slice(head, head + 1)
            fading = faded(on, log_col[:, pick], log_row[pick], rate_row[pick])
            systems.append(jnp.where(below, key_key * fading, 0.0))
            keys.append((key, scale))
    inverses = [eye - jnp.where(row // 2 == col // 2, system, 0.0) for system in systems]
    size = 2
    while size < length:
        lower = (row // (2 * size) == col // (2 * size)) & (row // size > col // size)
        crossing = [
            mm(jnp.where(lower, system, 0.0), inverse)
            for system, inverse in zip(systems, inverses)
        ]
        inverses = [
            inverse - mm(inverse, cross) for inverse, cross in zip(inverses, crossing)
        ]
        size *= 2
    targets = []
    for head in range(heads):
        key, scale = keys[head]
        lead = jnp.exp(log_col[:, head : head + 1])
        value = v_ref[:, head * DV : (head + 1) * DV].astype(F32)
        targets.append(jnp.concatenate([value, lead * scale * key.astype(F32)], axis=1))
    firsts = [mm(inverses[head], targets[head]) for head in range(heads)]
    missing = [
        targets[head] - firsts[head] - mm3(systems[head], firsts[head]) for head in range(heads)
    ]
    solutions = [firsts[head] + mm(inverses[head], missing[head]) for head in range(heads)]
    for head in range(heads):
        key, scale = keys[head]
        solved_ref[head] = solutions[head]
        last = log_col[length - 1 : length, head : head + 1]
        tail = jnp.exp(last - log_col[:, head : head + 1]) * rate_col[:, head : head + 1] * scale
        high, low = halves(solutions[head] * tail)
        written = mm(high, key, TN) + mm(low, key, TN)
        removed = written[DV:].astype(BF)
        added = written[:DV].astype(BF)
        fade = pieces(jnp.broadcast_to(jnp.exp(last), (MARKS, DK)))
        for cut in range(cuts):
            place = head * cuts + cut
            send_ref[place, :DK, :] = removed
            send_ref[place, DK : DK + rows, :] = added[cut * rows : (cut + 1) * rows]
            send_ref[place, DK + rows :, :] = fade


def inner_kernel(
    q_ref, k_ref, decay_ref, logit_ref, solved_ref, ids_ref, weight_ref, inside_ref, reach_ref, route_ref
):
    length = q_ref.shape[0]
    heads = decay_ref.shape[0]
    ratio = heads // (q_ref.shape[1] // DK)
    row, col = order(length)
    on = row >= col
    rate_row = 1.0 / (1.0 + jnp.exp(-logit_ref[...]))
    log_row, log_col = logs(decay_ref[...], on)
    for group in range(heads // ratio):
        part = slice(group * DK, (group + 1) * DK)
        query = q_ref[:, part]
        key = k_ref[:, part]
        query_f = query.astype(F32)
        query_scale = lax.rsqrt(jnp.sum(query_f * query_f, axis=1, keepdims=True) + EPS) * DK**-0.5
        _, scale_row = key_norms(key)
        query_key = mm(query, key, NT) * (query_scale * scale_row)
        for head in range(group * ratio, (group + 1) * ratio):
            pick = slice(head, head + 1)
            weight = query_key * faded(on, log_col[:, pick], log_row[pick], rate_row[pick])
            both = mm3(weight, solved_ref[head])
            inside_ref[head] = both[:, :DV]
            reach = jnp.exp(log_col[:, pick]) * query_scale * query_f - both[:, DV:]
            reach_ref[head] = reach.astype(BF)
    places, packed, _ = route_ref.shape
    targets = packed * 2 // 3
    number = lax.broadcasted_iota(jnp.int32, (targets, length), 0)
    number = (number // SHARES) * (places * SHARES) + number % SHARES
    for place in range(places):
        weight = jnp.zeros((targets, length), F32)
        for choice in range(ids_ref.shape[0]):
            hit = ids_ref[choice : choice + 1, :] == number + place * SHARES
            weight = weight + jnp.where(hit, weight_ref[choice : choice + 1, :], 0.0)
        weight = weight.astype(BF)
        route_ref[place, :targets, :] = weight[:, :DK]
        route_ref[place, targets:, :] = jnp.concatenate(
            [weight[: targets // 2, DK:], weight[targets // 2 :, DK:]], axis=1
        )


def total_kernel(got_ref, after_ref, total_ref):
    del after_ref
    blocks = got_ref.shape[0]
    rows = total_ref.shape[0] - DK - MARKS
    row = lax.broadcasted_iota(jnp.int32, (DK, DK), 0)
    col = lax.broadcasted_iota(jnp.int32, (DK, DK), 1)
    eye = jnp.where(row == col, 1.0, 0.0)
    whole = jnp.ones((1, DK), F32)
    product = eye
    state = jnp.zeros((rows, DK), F32)
    for block in range(blocks):
        removed, added, fade = unpack(got_ref[block], rows)
        if block == 0:
            product = fade * eye - removed.astype(F32)
            state = added
        else:
            product = advance(product, removed, fade)
            state = advance(state, removed, fade) + added
        whole = whole * fade
    total_ref[:DK, :] = (whole * eye - product).astype(BF)
    total_ref[DK : DK + rows, :] = state.astype(BF)
    total_ref[DK + rows :, :] = pieces(jnp.broadcast_to(whole, (MARKS, DK)))


def state_kernel(here_ref, got_ref, route_ref, *rest):
    totals, enter_ref = rest[:-1], rest[-1]
    blocks = enter_ref.shape[0]
    rows = enter_ref.shape[1] - route_ref.shape[1]
    enter_ref[:, rows:, :] = route_ref[...]
    state = jnp.zeros((rows, DK), F32)
    for distance in range(len(totals), 0, -1):
        removed, added, fade = unpack(totals[distance - 1], rows)
        state = jnp.where(distance <= here_ref[0], advance(state, removed, fade) + added, state)
    for block in range(blocks):
        enter_ref[block, :rows, :] = state.astype(BF)
        if block < blocks - 1:
            removed, added, fade = unpack(got_ref[block], rows)
            state = advance(state, removed, fade) + added


def output_kernel(
    here_ref, inside_ref, reach_ref, state_ref, gate_ref, gain_ref, proj_ref, gated_ref, give_ref
):
    heads = inside_ref.shape[0]
    gated = []
    for head in range(heads):
        part = slice(head * DV, (head + 1) * DV)
        cuts = state_ref.shape[0] // heads
        places = range(head * cuts, (head + 1) * cuts)
        state = jnp.concatenate([state_ref[place, : DV // cuts] for place in places], axis=0)
        output = inside_ref[head] + mm(reach_ref[head], state, NT)
        scaling = lax.rsqrt(jnp.mean(output * output, axis=1, keepdims=True) + EPS)
        opened = silu(gate_ref[:, part].astype(F32))
        gated.append((output * scaling * gain_ref[...] * opened).astype(BF))
    gated = jnp.concatenate(gated, axis=1)
    gated_ref[...] = gated
    columns, _, width = give_ref.shape
    for distance in range(columns):
        first = column_of(here_ref, distance, 1 - here_ref[3], columns, width)
        give_ref[distance] = mm(gated, proj_ref[:, pl.ds(first, width)]).astype(BF)


def column_of(here_ref, distance, core, columns, width):
    column = lax.rem(here_ref[2] + distance, columns)
    return pl.multiple_of((column * 2 + core) * width, width)


def keep_kernel(here_ref, gated_ref, proj_ref, rest_ref, keep_ref):
    gated = gated_ref[...]
    columns, _, width = keep_ref.shape
    for distance in range(columns):
        first = column_of(here_ref, distance, here_ref[3], columns, width)
        mixed = mm(gated, proj_ref[:, pl.ds(first, width)])
        if distance == 0:
            mixed = mixed + rest_ref[:, pl.ds(first, width)].astype(F32)
        keep_ref[distance] = mixed


def route_kernel(here_ref, got_ref, pick_ref, mix_ref):
    blocks, slots, length = pick_ref.shape
    targets = slots // SLOTS
    base = got_ref.shape[1] - targets - targets // 2
    iota = lambda shape, dim: lax.broadcasted_iota(jnp.int32, shape, dim)
    earlier = (iota((length, length), 0) > iota((length, length), 1)).astype(BF)
    earlier_t = (iota((length, length), 0) < iota((length, length), 1)).astype(BF)
    eye = (iota((length, length), 0) == iota((length, length), 1)).astype(BF)
    spread = (iota((targets, slots), 1) // SLOTS == iota((targets, slots), 0)).astype(BF)
    spread_t = (iota((slots, targets), 0) // SLOTS == iota((slots, targets), 1)).astype(BF)
    slot = (iota((length, slots), 1) % SLOTS).astype(F32)
    slot_t = (iota((slots, length), 0) % SLOTS).astype(F32)
    for block in range(blocks):
        source = lax.rem(here_ref[1] + blocks - block, blocks)
        first = got_ref[source, base : base + targets, :]
        last = got_ref[source, base + targets :, :]
        rest = length - DK
        last = jnp.concatenate([last[:, :rest], last[:, rest:]], axis=0)
        weight_t = jnp.concatenate([first, last], axis=1)
        named_t = weight_t.astype(F32) > 0.0
        weight = mm(eye, weight_t, NT)
        named = weight > 0.0
        place = jnp.where(named, mm(earlier, jnp.where(named, 1.0, 0.0)), -1.0)
        place_t = jnp.where(named_t, mm(jnp.where(named_t, 1.0, 0.0), earlier_t), -1.0)
        mix_ref[block] = jnp.where(mm(place, spread) == slot, mm(weight, spread), 0.0).astype(BF)
        pick_ref[block] = jnp.where(mm(spread_t, place_t) == slot_t, 1.0, 0.0).astype(BF)


def pick_kernel(pick_ref, *rest):
    tokens, send_ref = rest[:-1], rest[-1]
    targets = send_ref.shape[0]
    width = send_ref.shape[2]
    for block in range(pick_ref.shape[0]):
        rows = mm(pick_ref[block], tokens[block][...]).astype(BF)
        send_ref[:, block * SLOTS : (block + 1) * SLOTS, :] = rows.reshape(targets, SLOTS, width)


def expert_kernel(rows_ref, gain_ref, gate_ref, up_ref, down_ref, out_ref, normed_ref):
    groups, shares, count, width = rows_ref.shape
    for group in range(groups):
        place = slice(group * count, (group + 1) * count)
        total = jnp.zeros((count, 1), F32)
        for share in range(shares):
            piece = rows_ref[group, share].astype(F32)
            total = total + jnp.sum(piece * piece, axis=1, keepdims=True)
        scaling = lax.rsqrt(total / (shares * width) + EPS)
        for share in range(shares):
            part = slice(share * width, (share + 1) * width)
            piece = rows_ref[group, share].astype(F32)
            normed_ref[place, part] = (piece * scaling * gain_ref[:, part]).astype(BF)
    normed = normed_ref[...]
    hidden = (silu(mm(normed, gate_ref[...])) * mm(normed, up_ref[...])).astype(BF)
    for share in range(shares):
        part = slice(share * width, (share + 1) * width)
        produced = mm(hidden, down_ref[:, part]).astype(BF)
        for group in range(groups):
            out_ref[group, share] = produced[group * count : (group + 1) * count]


def combine_kernel(chosen, mix_ref, rows_ref, *outs):
    targets, _, width = rows_ref.shape
    for block, out_ref in zip(chosen, outs):
        rows = rows_ref[:, block * SLOTS : (block + 1) * SLOTS, :].reshape(targets * SLOTS, width)
        out_ref[...] = mm(mix_ref[block], rows).astype(out_ref.dtype)


SCALAR = pl.BlockSpec(memory_space=pltpu.SMEM)
VECTOR = pl.BlockSpec(memory_space=pltpu.VMEM)
UNREAD = pl.BlockSpec(memory_space=pl.ANY)
REMOTE = pl.BlockSpec(memory_space=pltpu.HBM)


def shifted(value, axis, distance):
    size = lax.axis_size(axis)
    return lax.ppermute(value, axis, [(i, (i + distance) % size) for i in range(size)])


def swap(value, axes):
    return lax.all_to_all(value, axes, 0, 0, tiled=True)


def spread_out(value, axis):
    right = [value, shifted(value, axis, 1), shifted(value, axis, 2)]
    left = [shifted(value, axis, -1), shifted(value, axis, -2)]
    far = shifted(left[1], axis, -2)
    left.append(shifted(left[1], axis, -1))
    right.append(shifted(right[2], axis, 1))
    left.append(far)
    return right + left[::-1]


def gathered_sum(parts, axis):
    def passed(value, distance):
        return shifted(value.astype(BF), axis, distance).astype(F32)

    left = parts[2] + passed(parts[4], -2) + passed(parts[3], -1)
    right = parts[6] + passed(parts[5], 1)
    right, first, last = lax.optimization_barrier((right, parts[1], parts[7]))
    near = passed(first, -1) + passed(last, 1)
    return parts[0] + near + (passed(left, -2) + passed(right, 2))


def on_device(
    query_in,
    key_in,
    value_in,
    gate_in,
    decay_rate,
    beta_logit,
    head_gain,
    out_proj,
    residual_in,
    post_gain,
    expert_ids,
    route_weight,
    w_gate,
    w_up,
    w_down,
):
    length = query_in.shape[0]
    heads = decay_rate.shape[0]
    blocks = lax.axis_size("z")
    groups = lax.axis_size("x")
    shares = lax.axis_size("y") * lax.axis_size("c")
    width = residual_in.shape[1] // shares
    count = blocks * SLOTS
    targets = groups * shares
    shape = jax.ShapeDtypeStruct

    rows = heads * DV // blocks
    extra = targets + targets // 2
    here = jnp.stack([lax.axis_index(axis) for axis in ("x", "z", "y", "c")])
    operands = (key_in, value_in, decay_rate, beta_logit)
    send, solved = call(
        solve_kernel,
        (
            shape((blocks, DK + rows + MARKS, DK), BF),
            shape((heads, length, DV + DK), F32),
        ),
        *operands,
        vmem=62,
        in_specs=[REMOTE] * len(operands),
        scratch_shapes=[pltpu.VMEM(item.shape, item.dtype) for item in operands]
        + [pltpu.SemaphoreType.DMA((len(operands),))],
    )
    got = swap(send, "z")
    inside, reach, route = call(
        inner_kernel,
        (
            shape((heads, length, DV), F32),
            shape((heads, length, DK), BF),
            shape((blocks, extra, DK), BF),
        ),
        query_in,
        key_in,
        decay_rate,
        beta_logit,
        solved,
        expert_ids.T,
        route_weight.T,
        vmem=16,
        flops=2 * 10**9,
        moved=3 * 10**6,
    )
    total = call(
        total_kernel,
        shape((DK + rows + MARKS, DK), BF),
        got,
        route,
        vmem=8,
        in_specs=[VECTOR, UNREAD],
    )
    totals = [shifted(total, "x", distance) for distance in range(1, groups)]
    enter = call(
        state_kernel,
        shape((blocks, rows + extra, DK), BF),
        here,
        got,
        route,
        *totals,
        vmem=8,
        in_specs=[SCALAR] + [VECTOR] * (2 + len(totals)),
    )
    back = swap(enter, "z")
    pick, mix = call(
        route_kernel,
        (
            shape((blocks, targets * SLOTS, length), BF),
            shape((blocks, length, targets * SLOTS), BF),
        ),
        here,
        back,
        vmem=12,
        flops=10**9,
        moved=4 * 10**6,
        in_specs=[SCALAR, VECTOR],
    )

    columns = lax.axis_size("y")
    gated, give = call(
        output_kernel,
        (shape((length, heads * DV), BF), shape((columns, length, width), BF)),
        here,
        inside,
        reach,
        back,
        gate_in,
        head_gain.reshape(1, DV),
        out_proj,
        vmem=16,
        in_specs=[SCALAR] + [VECTOR] * 6,
    )
    keep = call(
        keep_kernel,
        shape((columns, length, width), F32),
        here,
        gated,
        out_proj,
        residual_in,
        vmem=16,
        flops=2 * 10**8,
        moved=10**6,
        in_specs=[SCALAR] + [VECTOR] * 3,
    )
    both = keep + shifted(give, "c", 1).astype(F32)
    mixed = both[0]
    for distance in range(1, columns):
        mixed = mixed + shifted(both[distance].astype(BF), "y", distance).astype(F32)
    middle = mixed.astype(BF)

    tokens = spread_out(middle, "z")
    send = call(pick_kernel, shape((targets, count, width), BF), pick, *tokens, vmem=12)
    arrived = swap(send, ("x", "y", "c")).reshape(groups, shares, count, width)
    produced = call(
        expert_kernel,
        shape((groups, shares, count, width), BF),
        arrived,
        post_gain.reshape(1, -1),
        w_gate[0],
        w_up[0],
        w_down[0],
        vmem=24,
        scratch_shapes=[pltpu.VMEM((groups * count, shares * width), BF)],
    )
    returned = swap(produced.reshape(targets, count, width), ("x", "y", "c"))
    mixes = {}
    for chosen in ((4, 3, 5), (0, 1, 2, 6, 7)):
        outs = call(
            functools.partial(combine_kernel, chosen),
            tuple(shape((length, width), F32 if i in (0, 2, 6) else BF) for i in chosen),
            mix,
            returned,
            vmem=16,
            flops=10**8,
            moved=10**6,
        )
        mixes.update(zip(chosen, outs))
    expert_mix = gathered_sum(mixes, "z")
    layer_out = (middle.astype(F32) + expert_mix).astype(BF)
    return (middle, layer_out)


def solution(mesh):
    ctx, exp = mesh.devices.shape
    split = Mesh(mesh.devices.reshape(4, ctx // 4, exp // 2, 2), ("x", "z", "y", "c"))
    row, col = ("x", "z"), ("y", "c")
    in_specs = (
        P(row, col),
        P(row, col),
        P(row, col),
        P(row, col),
        P(col, row),
        P(col, row),
        P(),
        P(col, None),
        P(row, None),
        P(),
        P(row, None),
        P(row, None),
        P(row + col, None, None),
        P(row + col, None, None),
        P(row + col, None, None),
    )
    out_specs = (P(row, col), P(row, col))
    return jax.shard_map(
        on_device, mesh=split, in_specs=in_specs, out_specs=out_specs, check_vma=False
    )
```
